512 devices in a mesh: dp: 128 (over z, y_lo, x), head: 4 (over y_hi, core).
Axes of the slice: x: 4, y: 4 (y_hi: 2, y_lo: 2; y = y_hi * 2 + y_lo), z: 16, core: 2. Of those that a mesh axis runs over, the one named last changes fastest.
Arguments:
- queries: bfloat16 [128, 24, 512, 128], P('dp', None, 'head'), may hold values from -6.5 to 6.5
- key_rows: bfloat16 [128, 24, 512, 128], P('dp', None, 'head'), may hold values from -6.5 to 6.5
- value_rows: bfloat16 [128, 24, 512, 128], P('dp', None, 'head'), may hold values from -6 to 6
- upstream: bfloat16 [128, 24, 512, 128], P('dp', None, 'head'), may hold values from -24 to 24
- activations: bfloat16 [128, 512, 6144], P('dp', None, 'head'), may hold values from -14 to 14
Outputs:
- act_inv: bfloat16 [6144, 128], P(('head', 'dp'))
- grad_inv: bfloat16 [9216, 128], P(('head', 'dp'))
The draws below stay inside these ranges and needn't reach their ends.
All inputs are finite; a program needn't handle non-finite values.
Results may differ from the reference program's by a relative error of at most 0.0031.
The reference program's roundings to bfloat16 on the way count: a program that leaves them out, or rounds other values in their place, can miss the bound.
Values may be sent and summed in bfloat16 or wider, within the bound.
A program may use at most 64 MiB of HBM per device.

```python
import math
import jax
import jax.numpy as jnp
from jax import lax

D = 6144
HD = 128
LENGTH = 512
IMG = 128
HEADS = 24


def draw_queries(key, part):
    key = jax.random.fold_in(key, 11)
    full_shape = (IMG, HEADS, LENGTH, HD)
    values = jnp.clip(jax.random.normal(key, full_shape, jnp.float32), -4.0, 4.0)
    return values.astype(jnp.bfloat16)


def draw_key_rows(key, part):
    key = jax.random.fold_in(key, 13)
    full_shape = (IMG, HEADS, LENGTH, HD)
    values = jnp.clip(jax.random.normal(key, full_shape, jnp.float32), -4.0, 4.0)
    return values.astype(jnp.bfloat16)


def draw_upstream(key, part):
    key = jax.random.fold_in(key, 29)
    noise_key = jax.random.fold_in(key, 0)
    full_shape = (IMG, HEADS, LENGTH, HD)
    image_place = jnp.arange(IMG, dtype=jnp.float32).reshape(IMG, 1, 1, 1) / IMG
    values = jnp.clip(jax.random.normal(noise_key, full_shape, jnp.float32), -4.0, 4.0) * 3.0 ** image_place * 1.5
    return values.astype(jnp.bfloat16)


def draw_activations(key, part):
    key = jax.random.fold_in(key, 23)
    noise_key = jax.random.fold_in(key, 0)
    full_shape = (IMG, LENGTH, D)
    image_place = jnp.arange(IMG, dtype=jnp.float32).reshape(IMG, 1, 1) / IMG
    values = jnp.clip(jax.random.normal(noise_key, full_shape, jnp.float32), -4.0, 4.0) * 3.0 ** image_place * 0.6
    return values.astype(jnp.bfloat16)


def levels(own_key, shape, pieces, least, largest):
    loudness = 1.0
    for dim, shards_of in pieces:
        draws = jax.random.uniform(jax.random.fold_in(jax.random.fold_in(own_key, 6), dim), (shards_of,), jnp.float32, least / len(pieces), largest / len(pieces))
        loudness = loudness * jnp.repeat(jnp.exp(draws), shape[dim] // shards_of).reshape((-1,) + (1,) * (len(shape) - 1 - dim))
    return loudness


def noise(key, dims, spread, reach, cuts=(), kind=jnp.bfloat16):
    level = levels(key, dims, cuts, -0.22, 0.18) if cuts else 1.0
    entries = jax.random.normal(key, dims, jnp.float32) * spread * level
    return jnp.minimum(jnp.maximum(entries, -reach), reach).astype(kind)


def setup_inputs(seed: int = 0) -> dict:
    seeds = jax.random.split(jax.random.key(seed), 6)
    return {
        "queries": draw_queries(jax.random.fold_in(seeds[5], 71), 0),
        "key_rows": draw_key_rows(jax.random.fold_in(seeds[5], 71), 0),
        "value_rows": noise(seeds[2], (IMG, HEADS, LENGTH, HD), 1.0, 6.0, ((0, 128), (2, 4))),
        "upstream": draw_upstream(jax.random.fold_in(seeds[5], 71), 0),
        "activations": draw_activations(jax.random.fold_in(seeds[5], 71), 0),
    }


DAMPING = 0.1

def attend_back(queries, key_rows, value_rows, upstream):
    length, head_size = queries.shape
    block_rows = min(512, length)
    score_scale = 1.0 / math.sqrt(head_size)

    def one_block(partial_value, turn_index):
        key_grad, value_grad = partial_value
        first_row = turn_index * block_rows
        query_block = lax.dynamic_slice_in_dim(queries, first_row, block_rows, 0)
        upstream_block = lax.dynamic_slice_in_dim(upstream, first_row, block_rows, 0)
        scores = jnp.dot(query_block.astype(jnp.float32), key_rows.T.astype(jnp.float32), preferred_element_type=jnp.float32) * score_scale
        row_top = lax.optimization_barrier(jnp.max(scores, axis=1, keepdims=True))
        weights = jnp.exp(scores - row_top)
        probs_full = weights / lax.optimization_barrier(jnp.sum(weights, axis=1, keepdims=True))
        probs_half = probs_full.astype(jnp.bfloat16)
        output = jnp.dot(probs_half.astype(jnp.float32), value_rows.astype(jnp.float32), preferred_element_type=jnp.float32)
        row_delta = lax.optimization_barrier(jnp.sum(upstream_block.astype(jnp.float32) * output, axis=1, keepdims=True))
        probs_grad = jnp.dot(upstream_block.astype(jnp.float32), value_rows.T.astype(jnp.float32), preferred_element_type=jnp.float32)
        score_grad = (probs_full * (probs_grad - row_delta)).astype(jnp.bfloat16)
        query_grad = (jnp.dot(score_grad.astype(jnp.float32), key_rows.astype(jnp.float32), preferred_element_type=jnp.float32) * score_scale).astype(jnp.bfloat16)
        key_grad = key_grad + jnp.dot(score_grad.T.astype(jnp.float32), query_block.astype(jnp.float32), preferred_element_type=jnp.float32)
        value_grad = value_grad + jnp.dot(probs_half.T.astype(jnp.float32), upstream_block.astype(jnp.float32), preferred_element_type=jnp.float32)
        return ((key_grad, value_grad), query_grad)
    empty_grad = jnp.zeros((length, head_size), jnp.float32)
    partial_value, query_grad = lax.scan(one_block, (empty_grad, empty_grad), jnp.arange(length // block_rows))
    query_grad = query_grad.reshape(length, head_size)
    key_grad = (partial_value[0] * score_scale).astype(jnp.bfloat16)
    value_grad = partial_value[1].astype(jnp.bfloat16)
    return (query_grad, key_grad, value_grad)

def damped_inverse(gram_blocks):
    head_size = gram_blocks.shape[-1]
    trace_value = jnp.trace(gram_blocks, axis1=1, axis2=2)
    identity = jnp.eye(head_size, dtype=jnp.float32)
    damped = gram_blocks / (trace_value[:, None, None] / head_size + 1e-06) + DAMPING * identity
    lower_factor = jnp.linalg.cholesky(damped)
    identities = jnp.broadcast_to(identity, damped.shape)
    lower_inverse = lax.linalg.triangular_solve(lower_factor, identities, left_side=True, lower=True)
    return jnp.einsum('nkc,nkd->ncd', lower_inverse, lower_inverse, precision=lax.Precision.HIGHEST)

def reference(queries, key_rows, value_rows, upstream, activations):

    def per_head(head_items):
        return attend_back(head_items[0], head_items[1], head_items[2], head_items[3])

    def per_image(totals, image_items):
        grad_total, act_total = totals
        query_grad, key_grad, value_grad = lax.map(per_head, image_items[:4])
        grad_wide = jnp.stack([query_grad, key_grad, value_grad], 0).astype(jnp.float32)
        grad_total = grad_total + jnp.einsum('phlc,phld->hpcd', grad_wide, grad_wide, precision=lax.Precision.HIGHEST)
        acts_wide = image_items[4].reshape(LENGTH, D // HD, HD).astype(jnp.float32)
        act_total = act_total + jnp.einsum('tbc,tbd->bcd', acts_wide, acts_wide, precision=lax.Precision.HIGHEST)
        return ((grad_total, act_total), None)
    start = (jnp.zeros((HEADS, 3, HD, HD), jnp.float32), jnp.zeros((D // HD, HD, HD), jnp.float32))
    totals, unused = lax.scan(per_image, start, (queries, key_rows, value_rows, upstream, activations))
    grad_gram, act_gram = totals
    grad_inv = damped_inverse(grad_gram.reshape(HEADS * 3, HD, HD)).astype(jnp.bfloat16).reshape(HEADS * 3 * HD, HD)
    act_inv = damped_inverse(act_gram).astype(jnp.bfloat16).reshape(D, HD)
    return (act_inv, grad_inv)
```

```python
import math

import jax
import jax.numpy as jnp
from jax import lax
from jax.experimental import pallas as pl
from jax.experimental.pallas import tpu as pltpu
from jax.sharding import PartitionSpec as P

DAMPING = 0.1
XN, YN, ZN = 4, 2, 16
GROUP = XN * YN * ZN
HD = 128
LEN = 512
OWN = 6
QUERIES = 256
PANEL = 16
SLOTS = 8
SCALE = 1.0 / math.sqrt(HD)
LOG2E = 1.4426950408889634
MESH = pl.DeviceIdType.MESH
F32 = jnp.float32
BF16 = jnp.bfloat16


def dot(a, b, a_dim, b_dim):
    return lax.dot_general(a, b, (((a_dim,), (b_dim,)), ((), ())), preferred_element_type=F32)


def head_grams(rows):
    q, k, v, u = rows[0], rows[1], rows[2], rows[3]
    blocks = range(0, LEN, QUERIES)
    probs, probs_half = [], []
    for i in blocks:
        scores = dot(k, q[i : i + QUERIES], 1, 1)
        top = jnp.max(scores, axis=0, keepdims=True)
        weights = jnp.exp2((scores - top) * (SCALE * LOG2E))
        probs.append(weights * (1.0 / jnp.sum(weights, axis=0, keepdims=True)))
        probs_half.append(probs[-1].astype(BF16))
    probs_grad = [dot(v, u[i : i + QUERIES], 1, 1) for i in blocks]
    score_grad = []
    for full, half, grad in zip(probs, probs_half, probs_grad):
        row_delta = jnp.sum(half.astype(F32) * grad, axis=0, keepdims=True)
        score_grad.append((full * (grad - row_delta)).astype(BF16))
    value_grad = sum(dot(p, u[i : i + QUERIES], 1, 0) for p, i in zip(probs_half, blocks))
    value_grad = value_grad.astype(BF16)
    yield 2, dot(value_grad, value_grad, 0, 0)
    key_grad = sum(dot(g, q[i : i + QUERIES], 1, 0) for g, i in zip(score_grad, blocks))
    key_grad = (key_grad * SCALE).astype(BF16)
    yield 1, dot(key_grad, key_grad, 0, 0)
    query_grad = [(dot(k, g, 0, 0) * SCALE).astype(BF16) for g in score_grad]
    yield 0, sum(dot(g, g, 1, 1) for g in query_grad)


def invert_in_place(a_ref):
    lane = lax.broadcasted_iota(jnp.int32, (8, HD), 1)
    row = lax.broadcasted_iota(jnp.int32, (PANEL, HD), 0).reshape(PANEL // 8, 8, HD)
    done = lax.broadcasted_iota(jnp.int32, (HD, HD), 1) < PANEL

    def panel_step(panel, carry):
        rows = pl.ds(pl.multiple_of(panel * PANEL, PANEL), PANEL)
        full = a_ref[...]
        pivots = a_ref[rows, :].reshape(PANEL // 8, 8, HD)
        for s in range(0, PANEL, 2):
            g, r = s // 8, s % 8
            first, second = lane == s, lane == s + 1
            both = first | second

            def spread(i, j):
                return jnp.broadcast_to(
                    pivots[g, r + i : r + i + 1, s + j : s + j + 1], (8, HD)
                )

            a, b, d = spread(0, 0), spread(0, 1), spread(1, 1)
            inv = 1.0 / (a * d - b * b)
            row_a = jnp.broadcast_to(pivots[g, r : r + 1, :], (8, HD))
            row_b = jnp.broadcast_to(pivots[g, r + 1 : r + 2, :], (8, HD))
            row_a = jnp.where(first, 1.0, jnp.where(second, 0.0, row_a))
            row_b = jnp.where(first, 0.0, jnp.where(second, 1.0, row_b))
            new_a = (d * row_a - b * row_b) * inv
            new_b = (a * row_b - b * row_a) * inv
            others = (
                jnp.where(both[None], 0.0, pivots)
                - pivots[:, :, s : s + 1] * new_a[None]
                - pivots[:, :, s + 1 : s + 2] * new_b[None]
            )
            pivots = jnp.where(
                row == s, new_a[None], jnp.where(row == s + 1, new_b[None], others)
            )
        pivots = pivots.reshape(PANEL, HD)
        a_ref[...] = jnp.where(done, 0.0, full) - lax.dot_general(
            full[:, :PANEL], pivots, (((1,), (0,)), ((), ())),
            precision=lax.Precision.HIGHEST, preferred_element_type=F32,
        )
        a_ref[rows, :] = pivots
        a_ref[...] = pltpu.roll(a_ref[...], HD - PANEL, 1)
        return carry

    lax.fori_loop(0, HD // PANEL, panel_step, 0)


def whole_kernel(
    q_hbm, k_hbm, v_hbm, u_hbm, acts_hbm, act_out, grad_out,
    acts, buf, gram, x_in, x_sum, z_in, z_sum, parts, block, act_win, grad_win,
    acts_sem, buf_recv, core_send, far_send,
    xa_send, xg_send, x_recv, z_send, z_recv, g_send, g_recv, w_send, act_recv, grad_recv,
):
    tensors = (q_hbm, k_hbm, v_hbm, u_hbm)
    dp = lax.axis_index("dp")
    head = lax.axis_index("head")
    x = dp % XN
    y = (dp // XN) % YN
    z = dp // (XN * YN)
    core = head % 2
    half = head // 2

    def place(z_, y_, x_, head_):
        return (z_ * (XN * YN) + y_ * XN + x_, head_)

    def copy(src, dst, send, recv, device):
        return pltpu.make_async_remote_copy(
            src_ref=src, dst_ref=dst, send_sem=send, recv_sem=recv,
            device_id=device, device_id_type=MESH,
        )

    def wait_bytes(ref, sem):
        pltpu.make_async_copy(ref, ref, sem).wait()

    def rows_of(source):
        return pl.ds(pl.multiple_of(source * HD, HD), HD)

    def start_head(t):
        for i in range(4):
            for far in range(2):
                to = (1 - half) * 2 + far
                copy(
                    tensors[i].at[0, to * OWN + t], buf.at[t, i, rows_of(head), :],
                    far_send.at[t], buf_recv.at[t], place(z, y, x, to),
                ).start()
        other = half * 2 + 1 - core
        for i in range(4):
            copy(
                tensors[i].at[0, other * OWN + t], buf.at[t, i, rows_of(head), :],
                core_send.at[t], buf_recv.at[t], place(z, y, x, other),
            ).start()
            pltpu.make_async_copy(
                tensors[i].at[0, head * OWN + t], buf.at[t, i, rows_of(head), :],
                buf_recv.at[t],
            ).start()

    stage_slots = ((0, 3), (3, 3), (6, 1), (7, 1))

    def act_copy(r):
        to = (x + r) % XN
        return copy(
            gram.at[to, pl.ds(0, 3)], x_in.at[3 - r, pl.ds(0, 3)],
            xa_send.at[r - 1], x_recv.at[0], place(z, y, to, head),
        )

    def grad_place(t, p):
        n = 3 * t + p
        early = t < 4
        owner = jnp.where(early, n % XN, p)
        slot = jnp.where(early, 3 + n // XN, t + 2)
        stage = jnp.where(early, 1, t - 2)
        return n, owner, slot, stage

    def grad_copy(t, p):
        n, owner, slot, stage = grad_place(t, p)
        r = (x - owner + XN) % XN
        return owner, copy(
            gram.at[owner, slot], x_in.at[jnp.maximum(r - 1, 0), slot],
            xg_send.at[n], x_recv.at[stage], place(z, y, owner, head),
        )

    def compute_head(t):
        wait_bytes(buf.at[t], buf_recv.at[t])
        for p, block_gram in head_grams([buf[t, i] for i in range(4)]):
            unused, owner, slot, unused = grad_place(t, p)
            gram[owner, slot] = block_gram
            owner, send = grad_copy(t, p)
            pl.when(owner != x)(send.start)

    def z_piece(stage, to):
        first, count = stage_slots[stage]
        src = x_sum.at[pl.ds(first, count), pl.ds(pl.multiple_of(to * 8, 8), 8), :]
        return src, z_in.at[z, pl.ds(first, count)]

    def sum_x(stage):
        first, count = stage_slots[stage]
        slots = pl.ds(first, count)
        wait_bytes(x_in.at[:, slots], x_recv.at[stage])
        for s in range(first, first + count):
            x_sum[s] = (gram[x, s] + x_in[0, s]) + (x_in[1, s] + x_in[2, s])

        def send(to, carry):
            src, dst = z_piece(stage, to)

            @pl.when(to != z)
            def _():
                copy(
                    src, dst, z_send.at[stage], z_recv.at[stage], place(to, y, x, head)
                ).start()

            @pl.when(to == z)
            def _():
                pltpu.make_async_copy(src, dst, z_recv.at[stage]).start()

            return carry

        lax.fori_loop(0, ZN, send, 0)

    def sum_z(stage):
        first, count = stage_slots[stage]
        wait_bytes(z_in.at[:, pl.ds(first, count)], z_recv.at[stage])
        for s in range(first, first + count):
            z_sum[s] = jnp.sum(z_in[:, s], axis=0)
            dst = parts.at[y, pl.ds(pl.multiple_of(z * 8, 8), 8), :]
            mine = (z == 2 * s) & (y == 0)

            @pl.when(jnp.logical_not(mine))
            def _():
                copy(
                    z_sum.at[s], dst, g_send.at[s], g_recv, place(2 * s, 0, x, head)
                ).start()

            @pl.when(mine)
            def _():
                pltpu.make_async_copy(z_sum.at[s], dst, g_recv).start()

    late = x < 3

    def drain():
        def sent(t, carry):
            wait_bytes(buf.at[t, :, pl.ds(0, 2 * HD), :], far_send.at[t])
            wait_bytes(buf.at[t, :, pl.ds(0, HD), :], core_send.at[t])
            for p in range(3):
                owner, send = grad_copy(t, p)
                pl.when(owner != x)(send.wait_send)
            return carry

        lax.fori_loop(0, OWN, sent, 0)
        for r in (1, 3, 2):
            act_copy(r).wait_send()
        for stage, (first, count) in enumerate(stage_slots):
            def drain_stage():
                wait_bytes(z_in.at[pl.ds(0, ZN - 1), pl.ds(first, count)], z_send.at[stage])
                for s in range(first, first + count):
                    @pl.when(jnp.logical_not((z == 2 * s) & (y == 0)))
                    def _():
                        wait_bytes(z_sum.at[s], g_send.at[s])

            drain_stage() if stage < 2 else pl.when(late)(drain_stage)

    load = pltpu.make_async_copy(acts_hbm.at[0], acts, acts_sem)
    load.start()

    barrier = pltpu.get_barrier_semaphore()
    for r in range(1, 4):
        pl.semaphore_signal(
            barrier, inc=1, device_id=(dp, (head + r) % 4), device_id_type=MESH
        )

    def greet(r, carry):
        pl.semaphore_signal(
            barrier, inc=1, device_id=((dp + r) % GROUP, head), device_id_type=MESH
        )
        return carry

    lax.fori_loop(1, GROUP, greet, 0)
    pl.semaphore_wait(barrier, GROUP - 1 + 3)

    def start(t, carry):
        start_head(t)
        return carry

    lax.fori_loop(0, OWN, start, 0)
    load.wait()

    def act_gram(b, carry):
        item = acts[:, pl.ds(pl.multiple_of(b * HD, HD), HD)]
        gram[b // 3, b % 3] = dot(item, item, 0, 0)
        return carry

    lax.fori_loop(0, 12, act_gram, 0)
    for r in (2, 1, 3):
        act_copy(r).start()

    def step(t, carry):
        @pl.when(t == 3)
        def _():
            sum_x(0)

        @pl.when(t == 5)
        def _():
            sum_z(0)

        compute_head(t - 1)

        @pl.when(t == 5)
        def _():
            sum_x(1)

        return carry

    lax.fori_loop(1, OWN + 1, step, 0)
    pl.when(late)(lambda: sum_x(2))
    sum_z(1)
    pl.when(late)(lambda: sum_x(3))
    pl.when(late)(lambda: sum_z(2))
    pl.when(late)(lambda: sum_z(3))

    drain()
    slot = z // 2
    act_index = x * 3 + slot
    act_first = (act_index * 32) // 3
    grad_index = jnp.where(slot < 6, (slot - 3) * 4 + x, 12 + (slot - 6) * 3 + x)
    grad_first = (jnp.maximum(grad_index, 0) * 64) // 9
    inverter = (z % 2 == 0) & (y == 0) & ((slot < 6) | late)

    @pl.when(inverter)
    def _():
        wait_bytes(parts, g_recv)
        eye = lax.broadcasted_iota(jnp.int32, (HD, HD), 0) == lax.broadcasted_iota(
            jnp.int32, (HD, HD), 1
        )
        total = parts[0] + parts[1]
        trace = jnp.sum(jnp.where(eye, total, 0.0), axis=(0, 1), keepdims=True)
        block[...] = total / (trace / HD + 1e-06) + jnp.where(eye, DAMPING, 0.0)
        invert_in_place(block)


    def hand_out(block_index, first_to, count, pieces, window, recv, start):
        def one(i, carry):
            to = first_to + i
            for p in range(pieces):
                if pieces == 2:
                    piece = (3 * to) // 2 + p - 16 * block_index
                else:
                    piece = (9 * to) // 4 + p - 16 * block_index
                use = (piece >= 0) & (piece < 16)
                src = block.at[pl.ds(pl.multiple_of(piece * 8, 8), 8), :]
                dst = window.at[pl.ds(8 * p, 8), :]

                @pl.when(use & (to != dp))
                def _():
                    c = copy(src, dst, w_send.at[p, i], recv.at[p], (to, head))
                    c.start() if start else c.wait_send()

                if start:
                    @pl.when(use & (to == dp))
                    def _():
                        pltpu.make_async_copy(src, dst, recv.at[p]).start()

            return carry

        lax.fori_loop(0, count, one, 0)

    def each_piece(start):
        @pl.when(inverter & (slot < 3))
        def _():
            hand_out(act_index, act_first, 12, 2, act_win, act_recv, start)

        @pl.when(inverter & (slot >= 3))
        def _():
            hand_out(grad_index, grad_first, 9, 3, grad_win, grad_recv, start)

    each_piece(True)
    for s in range(2):
        wait_bytes(act_win.at[pl.ds(8 * s, 8), :], act_recv.at[s])
    for s in range(3):
        wait_bytes(grad_win.at[pl.ds(8 * s, 8), :], grad_recv.at[s])
    rows = act_win[...]
    act_out[...] = jnp.where(dp % 2 == 0, rows[0:12], rows[4:16]).astype(BF16)
    rows = grad_win[...]
    odd = dp % 4
    grad_out[...] = jnp.where(
        odd < 2,
        jnp.where(odd == 0, rows[0:18], rows[2:20]),
        jnp.where(odd == 2, rows[4:22], rows[6:24]),
    ).astype(BF16)

    each_piece(False)


def per_device(queries, key_rows, value_rows, upstream, activations):
    vmem = pl.BlockSpec(memory_space=pltpu.VMEM)
    hbm = pl.BlockSpec(memory_space=pltpu.HBM)
    dma = pltpu.SemaphoreType.DMA
    return pl.pallas_call(
        whole_kernel,
        out_shape=(
            jax.ShapeDtypeStruct((12, HD), BF16),
            jax.ShapeDtypeStruct((18, HD), BF16),
        ),
        in_specs=[hbm] * 5,
        out_specs=(vmem, vmem),
        scratch_shapes=[
            pltpu.VMEM((LEN, 12 * HD), BF16),
            pltpu.VMEM((OWN, 4, LEN, HD), BF16),
            pltpu.VMEM((XN, SLOTS, HD, HD), F32),
            pltpu.VMEM((XN - 1, SLOTS, HD, HD), F32),
            pltpu.VMEM((SLOTS, HD, HD), F32),
            pltpu.VMEM((ZN, SLOTS, 8, HD), F32),
            pltpu.VMEM((SLOTS, 8, HD), F32),
            pltpu.VMEM((YN, HD, HD), F32),
            pltpu.VMEM((HD, HD), F32),
            pltpu.VMEM((16, HD), F32),
            pltpu.VMEM((24, HD), F32),
            dma, dma((OWN,)), dma((OWN,)), dma((OWN,)),
            dma((3,)), dma((18,)), dma((4,)), dma((4,)), dma((4,)), dma((SLOTS,)), dma,
            dma((3, 12)), dma((2,)), dma((3,)),
        ],
        compiler_params=pltpu.CompilerParams(
            collective_id=0, has_side_effects=True, vmem_limit_bytes=62 * 1024 * 1024
        ),
        cost_estimate=pl.CostEstimate(
            flops=4_000_000_000, bytes_accessed=5_000_000, transcendentals=1_600_000
        ),
    )(queries, key_rows, value_rows, upstream, activations)


def solution(mesh):
    in_specs = (
        P("dp", None, "head", None),
        P("dp", None, "head", None),
        P("dp", None, "head", None),
        P("dp", None, "head", None),
        P("dp", None, "head"),
    )
    out_specs = (P(("head", "dp"), None), P(("head", "dp"), None))
    return jax.shard_map(
        per_device, mesh=mesh, in_specs=in_specs, out_specs=out_specs, check_vma=False
    )
```

```python
import math

import jax
import jax.numpy as jnp
from jax import lax
from jax.experimental import pallas as pl
from jax.experimental.pallas import tpu as pltpu
from jax.sharding import PartitionSpec as P

DAMPING = 0.1
XN, YN, ZN = 4, 2, 16
GROUP = XN * YN * ZN
HD = 128
LEN = 512
HALF = HD // 2
FOLDED = HALF + 8
PIECES = FOLDED // 8
OWN = 6
QUERIES = 256
PANEL = 16
SLOTS = 8
SCALE = 1.0 / math.sqrt(HD)
LOG2E = 1.4426950408889634
MESH = pl.DeviceIdType.MESH
F32 = jnp.float32
BF16 = jnp.bfloat16


def dot(a, b, a_dim, b_dim):
    return lax.dot_general(a, b, (((a_dim,), (b_dim,)), ((), ())), preferred_element_type=F32)


def head_grams(rows):
    q, k, v, u = rows[0], rows[1], rows[2], rows[3]
    blocks = range(0, LEN, QUERIES)
    probs, probs_half = [], []
    for i in blocks:
        scores = dot(k, q[i : i + QUERIES], 1, 1)
        top = jnp.max(scores, axis=0, keepdims=True)
        weights = jnp.exp2((scores - top) * (SCALE * LOG2E))
        probs.append(weights * (1.0 / jnp.sum(weights, axis=0, keepdims=True)))
        probs_half.append(probs[-1].astype(BF16))
    probs_grad = [dot(v, u[i : i + QUERIES], 1, 1) for i in blocks]
    score_grad = []
    for full, half, grad in zip(probs, probs_half, probs_grad):
        row_delta = jnp.sum(half.astype(F32) * grad, axis=0, keepdims=True)
        score_grad.append((full * (grad - row_delta)).astype(BF16))
    value_grad = sum(dot(p, u[i : i + QUERIES], 1, 0) for p, i in zip(probs_half, blocks))
    value_grad = value_grad.astype(BF16)
    yield 2, dot(value_grad, value_grad, 0, 0)
    key_grad = sum(dot(g, q[i : i + QUERIES], 1, 0) for g, i in zip(score_grad, blocks))
    key_grad = (key_grad * SCALE).astype(BF16)
    yield 1, dot(key_grad, key_grad, 0, 0)
    query_grad = [(dot(k, g, 0, 0) * SCALE).astype(BF16) for g in score_grad]
    yield 0, sum(dot(g, g, 1, 1) for g in query_grad)


def fold(block):
    row = lax.broadcasted_iota(jnp.int32, (HALF, HD), 0)
    lane = lax.broadcasted_iota(jnp.int32, (HALF, HD), 1)
    top, bottom = block[:HALF], pltpu.roll(block[HALF:], HALF, 1)
    mixed = jnp.where((lane < HALF) & (lane <= row), bottom, top)
    diagonal = jnp.sum(jnp.where(lane == row, top, 0.0), axis=0, keepdims=True)
    return mixed, jnp.broadcast_to(diagonal, (8, HD))


def unfold(mixed, diagonal):
    row = lax.broadcasted_iota(jnp.int32, (HALF, HD), 0)
    lane = lax.broadcasted_iota(jnp.int32, (HALF, HD), 1)
    turned = pltpu.roll(mixed, HALF, 1)
    upper = jnp.concatenate(
        [
            jnp.where((lane < HALF) & (lane <= row), 0.0, mixed),
            jnp.where((lane >= HALF) & (lane - HALF < row), turned, 0.0),
        ],
        0,
    )
    middle = jnp.concatenate(
        [
            jnp.where(lane == row, diagonal, 0.0),
            jnp.where(lane - HALF == row, turned, 0.0),
        ],
        0,
    )
    return upper + upper.T, middle


def invert_in_place(a_ref):
    lane = lax.broadcasted_iota(jnp.int32, (8, HD), 1)
    row = lax.broadcasted_iota(jnp.int32, (PANEL, HD), 0).reshape(PANEL // 8, 8, HD)
    done = lax.broadcasted_iota(jnp.int32, (HD, HD), 1) < PANEL

    def panel_step(panel, carry):
        rows = pl.ds(pl.multiple_of(panel * PANEL, PANEL), PANEL)
        full = a_ref[...]
        pivots = a_ref[rows, :].reshape(PANEL // 8, 8, HD)
        for s in range(0, PANEL, 2):
            g, r = s // 8, s % 8
            first, second = lane == s, lane == s + 1
            both = first | second

            def spread(i, j):
                return jnp.broadcast_to(
                    pivots[g, r + i : r + i + 1, s + j : s + j + 1], (8, HD)
                )

            a, b, d = spread(0, 0), spread(0, 1), spread(1, 1)
            inv = 1.0 / (a * d - b * b)
            row_a = jnp.broadcast_to(pivots[g, r : r + 1, :], (8, HD))
            row_b = jnp.broadcast_to(pivots[g, r + 1 : r + 2, :], (8, HD))
            row_a = jnp.where(first, 1.0, jnp.where(second, 0.0, row_a))
            row_b = jnp.where(first, 0.0, jnp.where(second, 1.0, row_b))
            new_a = (d * row_a - b * row_b) * inv
            new_b = (a * row_b - b * row_a) * inv
            others = (
                jnp.where(both[None], 0.0, pivots)
                - pivots[:, :, s : s + 1] * new_a[None]
                - pivots[:, :, s + 1 : s + 2] * new_b[None]
            )
            pivots = jnp.where(
                row == s, new_a[None], jnp.where(row == s + 1, new_b[None], others)
            )
        pivots = pivots.reshape(PANEL, HD)
        a_ref[...] = jnp.where(done, 0.0, full) - lax.dot_general(
            full[:, :PANEL], pivots, (((1,), (0,)), ((), ())),
            precision=lax.Precision.HIGHEST, preferred_element_type=F32,
        )
        a_ref[rows, :] = pivots
        a_ref[...] = pltpu.roll(a_ref[...], HD - PANEL, 1)
        return carry

    lax.fori_loop(0, HD // PANEL, panel_step, 0)


def whole_kernel(
    q_hbm, k_hbm, v_hbm, u_hbm, acts_hbm, act_out, grad_out,
    acts, buf, gram, x_in, x_sum, z_in, z_sum, parts, block, act_win, grad_win,
    acts_sem, buf_recv, core_send, far_send,
    xa_send, xg_send, x_recv, z_send, z_recv, g_send, g_recv, w_send, act_recv, grad_recv,
):
    tensors = (q_hbm, k_hbm, v_hbm, u_hbm)
    dp = lax.axis_index("dp")
    head = lax.axis_index("head")
    x = dp % XN
    y = (dp // XN) % YN
    z = dp // (XN * YN)
    core = head % 2
    half = head // 2

    def place(z_, y_, x_, head_):
        return (z_ * (XN * YN) + y_ * XN + x_, head_)

    def copy(src, dst, send, recv, device):
        return pltpu.make_async_remote_copy(
            src_ref=src, dst_ref=dst, send_sem=send, recv_sem=recv,
            device_id=device, device_id_type=MESH,
        )

    def wait_bytes(ref, sem):
        pltpu.make_async_copy(ref, ref, sem).wait()

    def rows_of(source):
        return pl.ds(pl.multiple_of(source * HD, HD), HD)

    def start_head(t):
        for i in range(4):
            for far in range(2):
                to = (1 - half) * 2 + far
                copy(
                    tensors[i].at[0, to * OWN + t], buf.at[t, i, rows_of(head), :],
                    far_send.at[t], buf_recv.at[t], place(z, y, x, to),
                ).start()
        other = half * 2 + 1 - core
        for i in range(4):
            copy(
                tensors[i].at[0, other * OWN + t], buf.at[t, i, rows_of(head), :],
                core_send.at[t], buf_recv.at[t], place(z, y, x, other),
            ).start()
            pltpu.make_async_copy(
                tensors[i].at[0, head * OWN + t], buf.at[t, i, rows_of(head), :],
                buf_recv.at[t],
            ).start()

    stage_slots = ((0, 3), (3, 3), (6, 1), (7, 1))

    def store_gram(owner, slot, value):
        mixed, diagonal = fold(value)
        gram[owner, slot, pl.ds(0, HALF)] = mixed
        gram[owner, slot, pl.ds(HALF, 8)] = diagonal

    def act_copy(r):
        to = (x + r) % XN
        return copy(
            gram.at[to, pl.ds(0, 3)], x_in.at[3 - r, pl.ds(0, 3)],
            xa_send.at[r - 1], x_recv.at[0], place(z, y, to, head),
        )

    def grad_place(t, p):
        n = 3 * t + p
        early = t < 4
        owner = jnp.where(early, n % XN, p)
        slot = jnp.where(early, 3 + n // XN, t + 2)
        stage = jnp.where(early, 1, t - 2)
        return n, owner, slot, stage

    def grad_copy(t, p):
        n, owner, slot, stage = grad_place(t, p)
        r = (x - owner + XN) % XN
        return owner, copy(
            gram.at[owner, slot], x_in.at[jnp.maximum(r - 1, 0), slot],
            xg_send.at[n], x_recv.at[stage], place(z, y, owner, head),
        )

    def compute_head(t):
        wait_bytes(buf.at[t], buf_recv.at[t])
        for p, block_gram in head_grams([buf[t, i] for i in range(4)]):
            unused, owner, slot, unused = grad_place(t, p)
            store_gram(owner, slot, block_gram)
            owner, send = grad_copy(t, p)
            pl.when(owner != x)(send.start)

    def piece_owner(j):
        return (ZN * j) // PIECES

    my_piece = (PIECES * z + PIECES - 1) // ZN
    holder = piece_owner(my_piece) == z

    def sum_x(stage):
        first, count = stage_slots[stage]
        slots = pl.ds(first, count)
        wait_bytes(x_in.at[:, slots], x_recv.at[stage])
        for s in range(first, first + count):
            x_sum[s] = (gram[x, s] + x_in[0, s]) + (x_in[1, s] + x_in[2, s])
        for j in range(PIECES):
            to = piece_owner(j)
            src, dst = x_sum.at[slots, pl.ds(8 * j, 8), :], z_in.at[z, slots]

            @pl.when(z != to)
            def _():
                copy(
                    src, dst, z_send.at[stage], z_recv.at[stage], place(to, y, x, head)
                ).start()

            @pl.when(z == to)
            def _():
                pltpu.make_async_copy(src, dst, z_recv.at[stage]).start()

    def sum_z(stage):
        first, count = stage_slots[stage]

        @pl.when(holder)
        def _():
            wait_bytes(z_in.at[:, pl.ds(first, count)], z_recv.at[stage])
            for s in range(first, first + count):
                z_sum[s] = jnp.sum(z_in[:, s], axis=0)
                dst = parts.at[y, pl.ds(pl.multiple_of(my_piece * 8, 8), 8), :]
                mine = (z == 2 * s) & (y == 0)

                @pl.when(jnp.logical_not(mine))
                def _():
                    copy(
                        z_sum.at[s], dst, g_send.at[s], g_recv, place(2 * s, 0, x, head)
                    ).start()

                @pl.when(mine)
                def _():
                    pltpu.make_async_copy(z_sum.at[s], dst, g_recv).start()

    late = x < 3

    def drain():
        def sent(t, carry):
            wait_bytes(buf.at[t, :, pl.ds(0, 2 * HD), :], far_send.at[t])
            wait_bytes(buf.at[t, :, pl.ds(0, HD), :], core_send.at[t])
            for p in range(3):
                owner, send = grad_copy(t, p)
                pl.when(owner != x)(send.wait_send)
            return carry

        lax.fori_loop(0, OWN, sent, 0)
        for r in (1, 3, 2):
            act_copy(r).wait_send()
        for stage, (first, count) in enumerate(stage_slots):
            def drain_stage():
                @pl.when(holder)
                def _():
                    wait_bytes(
                        z_in.at[pl.ds(0, PIECES - 1), pl.ds(first, count)], z_send.at[stage]
                    )
                    for s in range(first, first + count):
                        @pl.when(jnp.logical_not((z == 2 * s) & (y == 0)))
                        def _():
                            wait_bytes(z_sum.at[s], g_send.at[s])

                @pl.when(jnp.logical_not(holder))
                def _():
                    wait_bytes(z_in.at[pl.ds(0, PIECES), pl.ds(first, count)], z_send.at[stage])

            drain_stage() if stage < 2 else pl.when(late)(drain_stage)

    load = pltpu.make_async_copy(acts_hbm.at[0], acts, acts_sem)
    load.start()

    barrier = pltpu.get_barrier_semaphore()
    for r in range(1, 4):
        pl.semaphore_signal(
            barrier, inc=1, device_id=(dp, (head + r) % 4), device_id_type=MESH
        )

    def greet(r, carry):
        pl.semaphore_signal(
            barrier, inc=1, device_id=((dp + r) % GROUP, head), device_id_type=MESH
        )
        return carry

    lax.fori_loop(1, GROUP, greet, 0)
    pl.semaphore_wait(barrier, GROUP - 1 + 3)
    for t in range(3):
        start_head(t)
    load.wait()

    def act_gram(b, carry):
        item = acts[:, pl.ds(pl.multiple_of(b * HD, HD), HD)]
        store_gram(b // 3, b % 3, dot(item, item, 0, 0))
        return carry

    lax.fori_loop(0, 12, act_gram, 0)
    for r in (2, 1, 3):
        act_copy(r).start()

    def step(t, carry):
        @pl.when(t + 2 < OWN)
        def _():
            start_head(t + 2)

        @pl.when(t == 3)
        def _():
            sum_x(0)

        @pl.when(t == 5)
        def _():
            sum_z(0)

        compute_head(t - 1)

        @pl.when(t == 5)
        def _():
            sum_x(1)

        return carry

    lax.fori_loop(1, OWN + 1, step, 0)
    pl.when(late)(lambda: sum_x(2))
    sum_z(1)
    pl.when(late)(lambda: sum_x(3))
    pl.when(late)(lambda: sum_z(2))
    pl.when(late)(lambda: sum_z(3))

    drain()
    slot = z // 2
    act_index = x * 3 + slot
    act_first = (act_index * 32) // 3
    grad_index = jnp.where(slot < 6, (slot - 3) * 4 + x, 12 + (slot - 6) * 3 + x)
    grad_first = (jnp.maximum(grad_index, 0) * 64) // 9
    inverter = (z % 2 == 0) & (y == 0) & ((slot < 6) | late)

    @pl.when(inverter)
    def _():
        wait_bytes(parts, g_recv)
        eye = lax.broadcasted_iota(jnp.int32, (HD, HD), 0) == lax.broadcasted_iota(
            jnp.int32, (HD, HD), 1
        )
        total = parts[0] + parts[1]
        outside, middle = unfold(total[:HALF], total[HALF : HALF + 1])
        trace = jnp.sum(middle, axis=(0, 1), keepdims=True)
        block[...] = (outside + middle) / (trace / HD + 1e-06) + jnp.where(eye, DAMPING, 0.0)
        invert_in_place(block)


    def hand_out(block_index, first_to, count, pieces, window, recv, start):
        def one(i, carry):
            to = first_to + i
            for p in range(pieces):
                if pieces == 2:
                    piece = (3 * to) // 2 + p - 16 * block_index
                else:
                    piece = (9 * to) // 4 + p - 16 * block_index
                use = (piece >= 0) & (piece < 16)
                src = block.at[pl.ds(pl.multiple_of(piece * 8, 8), 8), :]
                dst = window.at[pl.ds(8 * p, 8), :]

                @pl.when(use & (to != dp))
                def _():
                    c = copy(src, dst, w_send.at[p, i], recv.at[p], (to, head))
                    c.start() if start else c.wait_send()

                if start:
                    @pl.when(use & (to == dp))
                    def _():
                        pltpu.make_async_copy(src, dst, recv.at[p]).start()

            return carry

        lax.fori_loop(0, count, one, 0)

    def each_piece(start):
        @pl.when(inverter & (slot < 3))
        def _():
            hand_out(act_index, act_first, 12, 2, act_win, act_recv, start)

        @pl.when(inverter & (slot >= 3))
        def _():
            hand_out(grad_index, grad_first, 9, 3, grad_win, grad_recv, start)

    each_piece(True)
    for s in range(2):
        wait_bytes(act_win.at[pl.ds(8 * s, 8), :], act_recv.at[s])
    for s in range(3):
        wait_bytes(grad_win.at[pl.ds(8 * s, 8), :], grad_recv.at[s])
    rows = act_win[...]
    act_out[...] = jnp.where(dp % 2 == 0, rows[0:12], rows[4:16]).astype(BF16)
    rows = grad_win[...]
    odd = dp % 4
    grad_out[...] = jnp.where(
        odd < 2,
        jnp.where(odd == 0, rows[0:18], rows[2:20]),
        jnp.where(odd == 2, rows[4:22], rows[6:24]),
    ).astype(BF16)

    each_piece(False)


def per_device(queries, key_rows, value_rows, upstream, activations):
    vmem = pl.BlockSpec(memory_space=pltpu.VMEM)
    hbm = pl.BlockSpec(memory_space=pltpu.HBM)
    dma = pltpu.SemaphoreType.DMA
    return pl.pallas_call(
        whole_kernel,
        out_shape=(
            jax.ShapeDtypeStruct((12, HD), BF16),
            jax.ShapeDtypeStruct((18, HD), BF16),
        ),
        in_specs=[hbm] * 5,
        out_specs=(vmem, vmem),
        scratch_shapes=[
            pltpu.VMEM((LEN, 12 * HD), BF16),
            pltpu.VMEM((OWN, 4, LEN, HD), BF16),
            pltpu.VMEM((XN, SLOTS, FOLDED, HD), F32),
            pltpu.VMEM((XN - 1, SLOTS, FOLDED, HD), F32),
            pltpu.VMEM((SLOTS, FOLDED, HD), F32),
            pltpu.VMEM((ZN, SLOTS, 8, HD), F32),
            pltpu.VMEM((SLOTS, 8, HD), F32),
            pltpu.VMEM((YN, FOLDED, HD), F32),
            pltpu.VMEM((HD, HD), F32),
            pltpu.VMEM((16, HD), F32),
            pltpu.VMEM((24, HD), F32),
            dma, dma((OWN,)), dma((OWN,)), dma((OWN,)),
            dma((3,)), dma((18,)), dma((4,)), dma((4,)), dma((4,)), dma((SLOTS,)), dma,
            dma((3, 12)), dma((2,)), dma((3,)),
        ],
        compiler_params=pltpu.CompilerParams(
            collective_id=0, has_side_effects=True, vmem_limit_bytes=62 * 1024 * 1024
        ),
        cost_estimate=pl.CostEstimate(
            flops=4_000_000_000, bytes_accessed=5_000_000, transcendentals=1_600_000
        ),
    )(queries, key_rows, value_rows, upstream, activations)


def solution(mesh):
    in_specs = (
        P("dp", None, "head", None),
        P("dp", None, "head", None),
        P("dp", None, "head", None),
        P("dp", None, "head", None),
        P("dp", None, "head"),
    )
    out_specs = (P(("head", "dp"), None), P(("head", "dp"), None))
    return jax.shard_map(
        per_device, mesh=mesh, in_specs=in_specs, out_specs=out_specs, check_vma=False
    )
```

```python
import math

import jax
import jax.numpy as jnp
from jax import lax
from jax.experimental import pallas as pl
from jax.experimental.pallas import tpu as pltpu
from jax.sharding import PartitionSpec as P

DAMPING = 0.1
XN, YN, ZN = 4, 2, 16
GROUP = XN * YN * ZN
HD = 128
LEN = 512
HALF = HD // 2
FOLDED = HALF + 8
PIECES = FOLDED // 8
OWN = 6
KEYS = 32
PANEL = 16
SLOTS = 8
SCALE = 1.0 / math.sqrt(HD)
LOG2E = 1.4426950408889634
MESH = pl.DeviceIdType.MESH
F32 = jnp.float32
BF16 = jnp.bfloat16


def dot(a, b, a_dim, b_dim):
    return lax.dot_general(a, b, (((a_dim,), (b_dim,)), ((), ())), preferred_element_type=F32)


def head_grams(rows, scores, probs_grad, probs_half, score_grad):
    q, k, v, u = rows[0], rows[1], rows[2], rows[3]
    pieces = [pl.ds(i, KEYS) for i in range(0, LEN, KEYS)]

    def rows_of_eight(piece):
        return piece.reshape(KEYS // 8, 8, LEN)

    scores[...] = dot(k, q, 1, 1)
    probs_grad[...] = dot(v, u, 1, 1)
    top = jnp.full((8, LEN), -jnp.inf, F32)
    for at in pieces:
        top = jnp.maximum(top, jnp.max(rows_of_eight(scores[at, :]), axis=0))
    top = jnp.max(top, axis=0, keepdims=True)
    total = jnp.zeros((8, LEN), F32)
    for at in pieces:
        weights = jnp.exp2((scores[at, :] - top) * (SCALE * LOG2E))
        scores[at, :] = weights
        total += jnp.sum(rows_of_eight(weights), axis=0)
    share = 1.0 / jnp.sum(total, axis=0, keepdims=True)
    row_delta = jnp.zeros((8, LEN), F32)
    for at in pieces:
        half = (scores[at, :] * share).astype(BF16)
        probs_half[at, :] = half
        row_delta += jnp.sum(rows_of_eight(half.astype(F32) * probs_grad[at, :]), axis=0)
    row_delta = jnp.sum(row_delta, axis=0, keepdims=True)
    for at in pieces:
        grad = scores[at, :] * share * (probs_grad[at, :] - row_delta)
        score_grad[at, :] = grad.astype(BF16)
    value_grad = dot(probs_half[...], u, 1, 0).astype(BF16)
    yield 2, dot(value_grad, value_grad, 0, 0)
    key_grad = (dot(score_grad[...], q, 1, 0) * SCALE).astype(BF16)
    yield 1, dot(key_grad, key_grad, 0, 0)
    query_grad = (dot(k, score_grad[...], 0, 0) * SCALE).astype(BF16)
    yield 0, dot(query_grad, query_grad, 1, 1)


def fold(block):
    row = lax.broadcasted_iota(jnp.int32, (HALF, HD), 0)
    lane = lax.broadcasted_iota(jnp.int32, (HALF, HD), 1)
    top, bottom = block[:HALF], pltpu.roll(block[HALF:], HALF, 1)
    mixed = jnp.where((lane < HALF) & (lane <= row), bottom, top)
    diagonal = jnp.sum(jnp.where(lane == row, top, 0.0), axis=0, keepdims=True)
    return mixed, jnp.broadcast_to(diagonal, (8, HD))


def unfold(mixed, diagonal):
    row = lax.broadcasted_iota(jnp.int32, (HALF, HD), 0)
    lane = lax.broadcasted_iota(jnp.int32, (HALF, HD), 1)
    turned = pltpu.roll(mixed, HALF, 1)
    upper = jnp.concatenate(
        [
            jnp.where((lane < HALF) & (lane <= row), 0.0, mixed),
            jnp.where((lane >= HALF) & (lane - HALF < row), turned, 0.0),
        ],
        0,
    )
    middle = jnp.concatenate(
        [
            jnp.where(lane == row, diagonal, 0.0),
            jnp.where(lane - HALF == row, turned, 0.0),
        ],
        0,
    )
    return upper + upper.T, middle


def invert_in_place(a_ref):
    lane = lax.broadcasted_iota(jnp.int32, (8, HD), 1)
    row = lax.broadcasted_iota(jnp.int32, (PANEL, HD), 0).reshape(PANEL // 8, 8, HD)
    done = lax.broadcasted_iota(jnp.int32, (HD, HD), 1) < PANEL

    def panel_step(panel, carry):
        rows = pl.ds(pl.multiple_of(panel * PANEL, PANEL), PANEL)
        full = a_ref[...]
        pivots = a_ref[rows, :].reshape(PANEL // 8, 8, HD)
        for s in range(0, PANEL, 2):
            g, r = s // 8, s % 8
            first, second = lane == s, lane == s + 1
            both = first | second

            def spread(i, j):
                return jnp.broadcast_to(
                    pivots[g, r + i : r + i + 1, s + j : s + j + 1], (8, HD)
                )

            a, b, d = spread(0, 0), spread(0, 1), spread(1, 1)
            inv = 1.0 / (a * d - b * b)
            row_a = jnp.broadcast_to(pivots[g, r : r + 1, :], (8, HD))
            row_b = jnp.broadcast_to(pivots[g, r + 1 : r + 2, :], (8, HD))
            row_a = jnp.where(first, 1.0, jnp.where(second, 0.0, row_a))
            row_b = jnp.where(first, 0.0, jnp.where(second, 1.0, row_b))
            new_a = (d * row_a - b * row_b) * inv
            new_b = (a * row_b - b * row_a) * inv
            others = (
                jnp.where(both[None], 0.0, pivots)
                - pivots[:, :, s : s + 1] * new_a[None]
                - pivots[:, :, s + 1 : s + 2] * new_b[None]
            )
            pivots = jnp.where(
                row == s, new_a[None], jnp.where(row == s + 1, new_b[None], others)
            )
        pivots = pivots.reshape(PANEL, HD)
        a_ref[...] = jnp.where(done, 0.0, full) - lax.dot_general(
            full[:, :PANEL], pivots, (((1,), (0,)), ((), ())),
            precision=lax.Precision.HIGHEST, preferred_element_type=F32,
        )
        a_ref[rows, :] = pivots
        a_ref[...] = pltpu.roll(a_ref[...], HD - PANEL, 1)
        return carry

    lax.fori_loop(0, HD // PANEL, panel_step, 0)


def whole_kernel(
    q_hbm, k_hbm, v_hbm, u_hbm, acts_hbm, act_out, grad_out,
    acts, buf, gram, x_in, x_sum, z_in, z_sum, parts, block, act_win, grad_win,
    acts_sem, buf_recv, core_send, far_send,
    xa_send, xg_send, x_recv, z_send, z_recv, g_send, g_recv, w_send, act_recv, grad_recv,
    *work,
):
    tensors = (q_hbm, k_hbm, v_hbm, u_hbm)
    dp = lax.axis_index("dp")
    head = lax.axis_index("head")
    x = dp % XN
    y = (dp // XN) % YN
    z = dp // (XN * YN)
    core = head % 2
    half = head // 2

    def place(z_, y_, x_, head_):
        return (z_ * (XN * YN) + y_ * XN + x_, head_)

    def copy(src, dst, send, recv, device):
        return pltpu.make_async_remote_copy(
            src_ref=src, dst_ref=dst, send_sem=send, recv_sem=recv,
            device_id=device, device_id_type=MESH,
        )

    def wait_bytes(ref, sem):
        pltpu.make_async_copy(ref, ref, sem).wait()

    def rows_of(source):
        return pl.ds(pl.multiple_of(source * HD, HD), HD)

    def start_head(t):
        for i in range(4):
            for far in range(2):
                to = (1 - half) * 2 + far
                copy(
                    tensors[i].at[0, to * OWN + t], buf.at[t, i, rows_of(head), :],
                    far_send.at[t], buf_recv.at[t], place(z, y, x, to),
                ).start()
        other = half * 2 + 1 - core
        for i in range(4):
            copy(
                tensors[i].at[0, other * OWN + t], buf.at[t, i, rows_of(head), :],
                core_send.at[t], buf_recv.at[t], place(z, y, x, other),
            ).start()
            pltpu.make_async_copy(
                tensors[i].at[0, head * OWN + t], buf.at[t, i, rows_of(head), :],
                buf_recv.at[t],
            ).start()

    stage_slots = ((0, 3), (3, 3), (6, 1), (7, 1))

    def store_gram(owner, slot, value):
        mixed, diagonal = fold(value)
        gram[owner, slot, pl.ds(0, HALF)] = mixed
        gram[owner, slot, pl.ds(HALF, 8)] = diagonal

    def act_copy(r):
        to = (x + r) % XN
        return copy(
            gram.at[to, pl.ds(0, 3)], x_in.at[3 - r, pl.ds(0, 3)],
            xa_send.at[r - 1], x_recv.at[0], place(z, y, to, head),
        )

    def grad_place(t, p):
        n = 3 * t + p
        early = t < 4
        owner = jnp.where(early, n % XN, p)
        slot = jnp.where(early, 3 + n // XN, t + 2)
        stage = jnp.where(early, 1, t - 2)
        return n, owner, slot, stage

    def grad_copy(t, p):
        n, owner, slot, stage = grad_place(t, p)
        r = (x - owner + XN) % XN
        return owner, copy(
            gram.at[owner, slot], x_in.at[jnp.maximum(r - 1, 0), slot],
            xg_send.at[n], x_recv.at[stage], place(z, y, owner, head),
        )

    def compute_head(t):
        wait_bytes(buf.at[t], buf_recv.at[t])
        for p, block_gram in head_grams([buf[t, i] for i in range(4)], *work):
            unused, owner, slot, unused = grad_place(t, p)
            store_gram(owner, slot, block_gram)
            owner, send = grad_copy(t, p)
            pl.when(owner != x)(send.start)

    def piece_owner(j):
        return (ZN * j) // PIECES

    my_piece = (PIECES * z + PIECES - 1) // ZN
    holder = piece_owner(my_piece) == z

    def sum_x(stage):
        first, count = stage_slots[stage]
        slots = pl.ds(first, count)
        wait_bytes(x_in.at[:, slots], x_recv.at[stage])
        for s in range(first, first + count):
            x_sum[s] = (gram[x, s] + x_in[0, s]) + (x_in[1, s] + x_in[2, s])
        for j in range(PIECES):
            to = piece_owner(j)
            src, dst = x_sum.at[slots, pl.ds(8 * j, 8), :], z_in.at[z, slots]

            @pl.when(z != to)
            def _():
                copy(
                    src, dst, z_send.at[stage], z_recv.at[stage], place(to, y, x, head)
                ).start()

            @pl.when(z == to)
            def _():
                pltpu.make_async_copy(src, dst, z_recv.at[stage]).start()

    def sum_z(stage):
        first, count = stage_slots[stage]

        @pl.when(holder)
        def _():
            wait_bytes(z_in.at[:, pl.ds(first, count)], z_recv.at[stage])
            for s in range(first, first + count):
                z_sum[s] = jnp.sum(z_in[:, s], axis=0)
                dst = parts.at[y, pl.ds(pl.multiple_of(my_piece * 8, 8), 8), :]
                mine = (z == 2 * s) & (y == 0)

                @pl.when(jnp.logical_not(mine))
                def _():
                    copy(
                        z_sum.at[s], dst, g_send.at[s], g_recv, place(2 * s, 0, x, head)
                    ).start()

                @pl.when(mine)
                def _():
                    pltpu.make_async_copy(z_sum.at[s], dst, g_recv).start()

    late = x < 3

    def drain():
        def sent(t, carry):
            wait_bytes(buf.at[t, :, pl.ds(0, 2 * HD), :], far_send.at[t])
            wait_bytes(buf.at[t, :, pl.ds(0, HD), :], core_send.at[t])
            for p in range(3):
                owner, send = grad_copy(t, p)
                pl.when(owner != x)(send.wait_send)
            return carry

        lax.fori_loop(0, OWN, sent, 0)
        for r in (1, 3, 2):
            act_copy(r).wait_send()
        for stage, (first, count) in enumerate(stage_slots):
            def drain_stage():
                @pl.when(holder)
                def _():
                    wait_bytes(
                        z_in.at[pl.ds(0, PIECES - 1), pl.ds(first, count)], z_send.at[stage]
                    )
                    for s in range(first, first + count):
                        @pl.when(jnp.logical_not((z == 2 * s) & (y == 0)))
                        def _():
                            wait_bytes(z_sum.at[s], g_send.at[s])

                @pl.when(jnp.logical_not(holder))
                def _():
                    wait_bytes(z_in.at[pl.ds(0, PIECES), pl.ds(first, count)], z_send.at[stage])

            drain_stage() if stage < 2 else pl.when(late)(drain_stage)

    load = pltpu.make_async_copy(acts_hbm.at[0], acts, acts_sem)
    load.start()

    barrier = pltpu.get_barrier_semaphore()
    for r in range(1, 4):
        pl.semaphore_signal(
            barrier, inc=1, device_id=(dp, (head + r) % 4), device_id_type=MESH
        )

    def greet(r, carry):
        pl.semaphore_signal(
            barrier, inc=1, device_id=((dp + r) % GROUP, head), device_id_type=MESH
        )
        return carry

    lax.fori_loop(1, GROUP, greet, 0)
    pl.semaphore_wait(barrier, GROUP - 1 + 3)
    for t in range(3):
        start_head(t)
    load.wait()

    def act_gram(b, carry):
        item = acts[:, pl.ds(pl.multiple_of(b * HD, HD), HD)]
        store_gram(b // 3, b % 3, dot(item, item, 0, 0))
        return carry

    lax.fori_loop(0, 12, act_gram, 0)
    for r in (2, 1, 3):
        act_copy(r).start()

    def step(t, carry):
        @pl.when(t + 2 < OWN)
        def _():
            start_head(t + 2)

        @pl.when(t == 3)
        def _():
            sum_x(0)

        @pl.when(t == 5)
        def _():
            sum_z(0)

        compute_head(t - 1)

        @pl.when(t == 5)
        def _():
            sum_x(1)

        return carry

    lax.fori_loop(1, OWN + 1, step, 0)
    pl.when(late)(lambda: sum_x(2))
    sum_z(1)
    pl.when(late)(lambda: sum_x(3))
    pl.when(late)(lambda: sum_z(2))
    pl.when(late)(lambda: sum_z(3))

    drain()
    slot = z // 2
    act_index = x * 3 + slot
    act_first = (act_index * 32) // 3
    grad_index = jnp.where(slot < 6, (slot - 3) * 4 + x, 12 + (slot - 6) * 3 + x)
    grad_first = (jnp.maximum(grad_index, 0) * 64) // 9
    inverter = (z % 2 == 0) & (y == 0) & ((slot < 6) | late)

    @pl.when(inverter)
    def _():
        wait_bytes(parts, g_recv)
        eye = lax.broadcasted_iota(jnp.int32, (HD, HD), 0) == lax.broadcasted_iota(
            jnp.int32, (HD, HD), 1
        )
        total = parts[0] + parts[1]
        outside, middle = unfold(total[:HALF], total[HALF : HALF + 1])
        trace = jnp.sum(middle, axis=(0, 1), keepdims=True)
        block[...] = (outside + middle) / (trace / HD + 1e-06) + jnp.where(eye, DAMPING, 0.0)
        invert_in_place(block)


    def hand_out(block_index, first_to, count, pieces, window, recv, start):
        def one(i, carry):
            to = first_to + i
            for p in range(pieces):
                if pieces == 2:
                    piece = (3 * to) // 2 + p - 16 * block_index
                else:
                    piece = (9 * to) // 4 + p - 16 * block_index
                use = (piece >= 0) & (piece < 16)
                src = block.at[pl.ds(pl.multiple_of(piece * 8, 8), 8), :]
                dst = window.at[pl.ds(8 * p, 8), :]

                @pl.when(use & (to != dp))
                def _():
                    c = copy(src, dst, w_send.at[p, i], recv.at[p], (to, head))
                    c.start() if start else c.wait_send()

                if start:
                    @pl.when(use & (to == dp))
                    def _():
                        pltpu.make_async_copy(src, dst, recv.at[p]).start()

            return carry

        lax.fori_loop(0, count, one, 0)

    def each_piece(start):
        @pl.when(inverter & (slot < 3))
        def _():
            hand_out(act_index, act_first, 12, 2, act_win, act_recv, start)

        @pl.when(inverter & (slot >= 3))
        def _():
            hand_out(grad_index, grad_first, 9, 3, grad_win, grad_recv, start)

    each_piece(True)
    for s in range(2):
        wait_bytes(act_win.at[pl.ds(8 * s, 8), :], act_recv.at[s])
    for s in range(3):
        wait_bytes(grad_win.at[pl.ds(8 * s, 8), :], grad_recv.at[s])
    rows = act_win[...]
    act_out[...] = jnp.where(dp % 2 == 0, rows[0:12], rows[4:16]).astype(BF16)
    rows = grad_win[...]
    odd = dp % 4
    grad_out[...] = jnp.where(
        odd < 2,
        jnp.where(odd == 0, rows[0:18], rows[2:20]),
        jnp.where(odd == 2, rows[4:22], rows[6:24]),
    ).astype(BF16)

    each_piece(False)


def per_device(queries, key_rows, value_rows, upstream, activations):
    vmem = pl.BlockSpec(memory_space=pltpu.VMEM)
    hbm = pl.BlockSpec(memory_space=pltpu.HBM)
    dma = pltpu.SemaphoreType.DMA
    return pl.pallas_call(
        whole_kernel,
        out_shape=(
            jax.ShapeDtypeStruct((12, HD), BF16),
            jax.ShapeDtypeStruct((18, HD), BF16),
        ),
        in_specs=[hbm] * 5,
        out_specs=(vmem, vmem),
        scratch_shapes=[
            pltpu.VMEM((LEN, 12 * HD), BF16),
            pltpu.VMEM((OWN, 4, LEN, HD), BF16),
            pltpu.VMEM((XN, SLOTS, FOLDED, HD), F32),
            pltpu.VMEM((XN - 1, SLOTS, FOLDED, HD), F32),
            pltpu.VMEM((SLOTS, FOLDED, HD), F32),
            pltpu.VMEM((ZN, SLOTS, 8, HD), F32),
            pltpu.VMEM((SLOTS, 8, HD), F32),
            pltpu.VMEM((YN, FOLDED, HD), F32),
            pltpu.VMEM((HD, HD), F32),
            pltpu.VMEM((16, HD), F32),
            pltpu.VMEM((24, HD), F32),
            dma, dma((OWN,)), dma((OWN,)), dma((OWN,)),
            dma((3,)), dma((18,)), dma((4,)), dma((4,)), dma((4,)), dma((SLOTS,)), dma,
            dma((3, 12)), dma((2,)), dma((3,)),
            pltpu.VMEM((LEN, LEN), F32),
            pltpu.VMEM((LEN, LEN), F32),
            pltpu.VMEM((LEN, LEN), BF16),
            pltpu.VMEM((LEN, LEN), BF16),
        ],
        compiler_params=pltpu.CompilerParams(
            collective_id=0, has_side_effects=True, vmem_limit_bytes=62 * 1024 * 1024
        ),
        cost_estimate=pl.CostEstimate(
            flops=4_000_000_000, bytes_accessed=5_000_000, transcendentals=1_600_000
        ),
    )(queries, key_rows, value_rows, upstream, activations)


def solution(mesh):
    in_specs = (
        P("dp", None, "head", None),
        P("dp", None, "head", None),
        P("dp", None, "head", None),
        P("dp", None, "head", None),
        P("dp", None, "head"),
    )
    out_specs = (P(("head", "dp"), None), P(("head", "dp"), None))
    return jax.shard_map(
        per_device, mesh=mesh, in_specs=in_specs, out_specs=out_specs, check_vma=False
    )
```

```python
import math

import jax
import jax.numpy as jnp
from jax import lax
from jax.experimental import pallas as pl
from jax.experimental.pallas import tpu as pltpu
from jax.sharding import PartitionSpec as P

DAMPING = 0.1
XN, YN, ZN = 4, 2, 16
GROUP = XN * YN * ZN
HD = 128
LEN = 512
HALF = HD // 2
FOLDED = HALF + 8
PIECES = FOLDED // 8
OWN = 6
QUERIES = 256
PANEL = 32
SLOTS = 8
SCALE = 1.0 / math.sqrt(HD)
LOG2E = 1.4426950408889634
MESH = pl.DeviceIdType.MESH
F32 = jnp.float32
BF16 = jnp.bfloat16


def dot(a, b, a_dim, b_dim):
    return lax.dot_general(a, b, (((a_dim,), (b_dim,)), ((), ())), preferred_element_type=F32)


def head_grams(rows):
    q, k, v, u = rows[0], rows[1], rows[2], rows[3]
    blocks = range(0, LEN, QUERIES)
    probs, probs_half = [], []
    for i in blocks:
        scores = dot(k, q[i : i + QUERIES], 1, 1)
        top = jnp.max(scores, axis=0, keepdims=True)
        weights = jnp.exp2((scores - top) * (SCALE * LOG2E))
        probs.append(weights * (1.0 / jnp.sum(weights, axis=0, keepdims=True)))
        probs_half.append(probs[-1].astype(BF16))
    probs_grad = [dot(v, u[i : i + QUERIES], 1, 1) for i in blocks]
    score_grad = []
    for full, half, grad in zip(probs, probs_half, probs_grad):
        row_delta = jnp.sum(half.astype(F32) * grad, axis=0, keepdims=True)
        score_grad.append((full * (grad - row_delta)).astype(BF16))
    value_grad = sum(dot(p, u[i : i + QUERIES], 1, 0) for p, i in zip(probs_half, blocks))
    value_grad = value_grad.astype(BF16)
    yield 2, dot(value_grad, value_grad, 0, 0)
    key_grad = sum(dot(g, q[i : i + QUERIES], 1, 0) for g, i in zip(score_grad, blocks))
    key_grad = (key_grad * SCALE).astype(BF16)
    yield 1, dot(key_grad, key_grad, 0, 0)
    query_grad = [(dot(k, g, 0, 0) * SCALE).astype(BF16) for g in score_grad]
    yield 0, sum(dot(g, g, 1, 1) for g in query_grad)


def fold(block):
    row = lax.broadcasted_iota(jnp.int32, (HALF, HD), 0)
    lane = lax.broadcasted_iota(jnp.int32, (HALF, HD), 1)
    top, bottom = block[:HALF], pltpu.roll(block[HALF:], HALF, 1)
    mixed = jnp.where((lane < HALF) & (lane <= row), bottom, top)
    diagonal = jnp.sum(jnp.where(lane == row, top, 0.0), axis=0, keepdims=True)
    return mixed, jnp.broadcast_to(diagonal, (8, HD))


def unfold(mixed, diagonal):
    row = lax.broadcasted_iota(jnp.int32, (HALF, HD), 0)
    lane = lax.broadcasted_iota(jnp.int32, (HALF, HD), 1)
    turned = pltpu.roll(mixed, HALF, 1)
    upper = jnp.concatenate(
        [
            jnp.where((lane < HALF) & (lane <= row), 0.0, mixed),
            jnp.where((lane >= HALF) & (lane - HALF < row), turned, 0.0),
        ],
        0,
    )
    middle = jnp.concatenate(
        [
            jnp.where(lane == row, diagonal, 0.0),
            jnp.where(lane - HALF == row, turned, 0.0),
        ],
        0,
    )
    return upper + upper.T, middle


def invert_in_place(a_ref):
    lane = lax.broadcasted_iota(jnp.int32, (8, HD), 1)
    row = lax.broadcasted_iota(jnp.int32, (PANEL, HD), 0).reshape(PANEL // 8, 8, HD)
    done = lax.broadcasted_iota(jnp.int32, (HD, HD), 1) < PANEL

    def panel_step(panel, carry):
        rows = pl.ds(pl.multiple_of(panel * PANEL, PANEL), PANEL)
        full = a_ref[...]
        pivots = a_ref[rows, :].reshape(PANEL // 8, 8, HD)
        for s in range(0, PANEL, 2):
            g, r = s // 8, s % 8
            first, second = lane == s, lane == s + 1
            both = first | second

            def spread(i, j):
                return jnp.broadcast_to(
                    pivots[g, r + i : r + i + 1, s + j : s + j + 1], (8, HD)
                )

            a, b, d = spread(0, 0), spread(0, 1), spread(1, 1)
            inv = 1.0 / (a * d - b * b)
            row_a = jnp.broadcast_to(pivots[g, r : r + 1, :], (8, HD))
            row_b = jnp.broadcast_to(pivots[g, r + 1 : r + 2, :], (8, HD))
            row_a = jnp.where(first, 1.0, jnp.where(second, 0.0, row_a))
            row_b = jnp.where(first, 0.0, jnp.where(second, 1.0, row_b))
            new_a = (d * row_a - b * row_b) * inv
            new_b = (a * row_b - b * row_a) * inv
            others = (
                jnp.where(both[None], 0.0, pivots)
                - pivots[:, :, s : s + 1] * new_a[None]
                - pivots[:, :, s + 1 : s + 2] * new_b[None]
            )
            pivots = jnp.where(
                row == s, new_a[None], jnp.where(row == s + 1, new_b[None], others)
            )
        pivots = pivots.reshape(PANEL, HD)
        a_ref[...] = jnp.where(done, 0.0, full) - lax.dot_general(
            full[:, :PANEL], pivots, (((1,), (0,)), ((), ())),
            precision=lax.Precision.HIGHEST, preferred_element_type=F32,
        )
        a_ref[rows, :] = pivots
        a_ref[...] = pltpu.roll(a_ref[...], HD - PANEL, 1)
        return carry

    lax.fori_loop(0, HD // PANEL, panel_step, 0)


def whole_kernel(
    q_hbm, k_hbm, v_hbm, u_hbm, acts_hbm, act_out, grad_out,
    acts, buf, gram, x_in, x_sum, z_in, z_sum, parts, block, act_win, grad_win,
    acts_sem, buf_recv, core_send, far_send,
    xa_send, xg_send, x_recv, z_send, z_recv, g_send, g_recv, w_send, act_recv, grad_recv,
):
    tensors = (q_hbm, k_hbm, v_hbm, u_hbm)
    dp = lax.axis_index("dp")
    head = lax.axis_index("head")
    x = dp % XN
    y = (dp // XN) % YN
    z = dp // (XN * YN)
    core = head % 2
    half = head // 2

    def place(z_, y_, x_, head_):
        return (z_ * (XN * YN) + y_ * XN + x_, head_)

    def copy(src, dst, send, recv, device):
        return pltpu.make_async_remote_copy(
            src_ref=src, dst_ref=dst, send_sem=send, recv_sem=recv,
            device_id=device, device_id_type=MESH,
        )

    def wait_bytes(ref, sem):
        pltpu.make_async_copy(ref, ref, sem).wait()

    def rows_of(source):
        return pl.ds(pl.multiple_of(source * HD, HD), HD)

    def start_head(t):
        for i in range(4):
            for far in range(2):
                to = (1 - half) * 2 + far
                copy(
                    tensors[i].at[0, to * OWN + t], buf.at[t, i, rows_of(head), :],
                    far_send.at[t], buf_recv.at[t], place(z, y, x, to),
                ).start()
        other = half * 2 + 1 - core
        for i in range(4):
            copy(
                tensors[i].at[0, other * OWN + t], buf.at[t, i, rows_of(head), :],
                core_send.at[t], buf_recv.at[t], place(z, y, x, other),
            ).start()
            pltpu.make_async_copy(
                tensors[i].at[0, head * OWN + t], buf.at[t, i, rows_of(head), :],
                buf_recv.at[t],
            ).start()

    stage_slots = ((0, 3), (3, 3), (6, 1), (7, 1))

    def store_gram(owner, slot, value):
        mixed, diagonal = fold(value)
        gram[owner, slot, pl.ds(0, HALF)] = mixed
        gram[owner, slot, pl.ds(HALF, 8)] = diagonal

    def act_copy(r):
        to = (x + r) % XN
        return copy(
            gram.at[to, pl.ds(0, 3)], x_in.at[3 - r, pl.ds(0, 3)],
            xa_send.at[r - 1], x_recv.at[0], place(z, y, to, head),
        )

    def grad_place(t, p):
        n = 3 * t + p
        early = t < 4
        owner = jnp.where(early, n % XN, p)
        slot = jnp.where(early, 3 + n // XN, t + 2)
        stage = jnp.where(early, 1, t - 2)
        return n, owner, slot, stage

    def grad_copy(t, p):
        n, owner, slot, stage = grad_place(t, p)
        r = (x - owner + XN) % XN
        return owner, copy(
            gram.at[owner, slot], x_in.at[jnp.maximum(r - 1, 0), slot],
            xg_send.at[n], x_recv.at[stage], place(z, y, owner, head),
        )

    def compute_head(t):
        wait_bytes(buf.at[t], buf_recv.at[t])
        for p, block_gram in head_grams([buf[t, i] for i in range(4)]):
            unused, owner, slot, unused = grad_place(t, p)
            store_gram(owner, slot, block_gram)
            owner, send = grad_copy(t, p)
            pl.when(owner != x)(send.start)

    def piece_owner(j):
        return (ZN * j) // PIECES

    my_piece = (PIECES * z + PIECES - 1) // ZN
    holder = piece_owner(my_piece) == z

    def sum_x(stage):
        first, count = stage_slots[stage]
        slots = pl.ds(first, count)
        wait_bytes(x_in.at[:, slots], x_recv.at[stage])
        for s in range(first, first + count):
            x_sum[s] = (gram[x, s] + x_in[0, s]) + (x_in[1, s] + x_in[2, s])
        for j in range(PIECES):
            to = piece_owner(j)
            src, dst = x_sum.at[slots, pl.ds(8 * j, 8), :], z_in.at[z, slots]

            @pl.when(z != to)
            def _():
                copy(
                    src, dst, z_send.at[stage], z_recv.at[stage], place(to, y, x, head)
                ).start()

            @pl.when(z == to)
            def _():
                pltpu.make_async_copy(src, dst, z_recv.at[stage]).start()

    def sum_z(stage):
        first, count = stage_slots[stage]

        @pl.when(holder)
        def _():
            wait_bytes(z_in.at[:, pl.ds(first, count)], z_recv.at[stage])
            for s in range(first, first + count):
                z_sum[s] = jnp.sum(z_in[:, s], axis=0)
                dst = parts.at[y, pl.ds(pl.multiple_of(my_piece * 8, 8), 8), :]
                mine = (z == 2 * s) & (y == 0)

                @pl.when(jnp.logical_not(mine))
                def _():
                    copy(
                        z_sum.at[s], dst, g_send.at[s], g_recv, place(2 * s, 0, x, head)
                    ).start()

                @pl.when(mine)
                def _():
                    pltpu.make_async_copy(z_sum.at[s], dst, g_recv).start()

    late = x < 3

    def drain():
        def sent(t, carry):
            wait_bytes(buf.at[t, :, pl.ds(0, 2 * HD), :], far_send.at[t])
            wait_bytes(buf.at[t, :, pl.ds(0, HD), :], core_send.at[t])
            for p in range(3):
                owner, send = grad_copy(t, p)
                pl.when(owner != x)(send.wait_send)
            return carry

        lax.fori_loop(0, OWN, sent, 0)
        for r in (1, 3, 2):
            act_copy(r).wait_send()
        for stage, (first, count) in enumerate(stage_slots):
            def drain_stage():
                @pl.when(holder)
                def _():
                    wait_bytes(
                        z_in.at[pl.ds(0, PIECES - 1), pl.ds(first, count)], z_send.at[stage]
                    )
                    for s in range(first, first + count):
                        @pl.when(jnp.logical_not((z == 2 * s) & (y == 0)))
                        def _():
                            wait_bytes(z_sum.at[s], g_send.at[s])

                @pl.when(jnp.logical_not(holder))
                def _():
                    wait_bytes(z_in.at[pl.ds(0, PIECES), pl.ds(first, count)], z_send.at[stage])

            drain_stage() if stage < 2 else pl.when(late)(drain_stage)

    load = pltpu.make_async_copy(acts_hbm.at[0], acts, acts_sem)
    load.start()

    barrier = pltpu.get_barrier_semaphore()
    for r in range(1, 4):
        pl.semaphore_signal(
            barrier, inc=1, device_id=(dp, (head + r) % 4), device_id_type=MESH
        )

    def greet(r, carry):
        pl.semaphore_signal(
            barrier, inc=1, device_id=((dp + r) % GROUP, head), device_id_type=MESH
        )
        return carry

    lax.fori_loop(1, GROUP, greet, 0)
    pl.semaphore_wait(barrier, GROUP - 1 + 3)
    for t in range(3):
        start_head(t)
    load.wait()

    def act_gram(b, carry):
        item = acts[:, pl.ds(pl.multiple_of(b * HD, HD), HD)]
        store_gram(b // 3, b % 3, dot(item, item, 0, 0))
        return carry

    lax.fori_loop(0, 12, act_gram, 0)
    for r in (2, 1, 3):
        act_copy(r).start()

    def step(t, carry):
        @pl.when(t + 2 < OWN)
        def _():
            start_head(t + 2)

        @pl.when(t == 3)
        def _():
            sum_x(0)

        @pl.when(t == 5)
        def _():
            sum_z(0)

        compute_head(t - 1)

        @pl.when(t == 5)
        def _():
            sum_x(1)

        return carry

    lax.fori_loop(1, OWN + 1, step, 0)
    pl.when(late)(lambda: sum_x(2))
    sum_z(1)
    pl.when(late)(lambda: sum_x(3))
    pl.when(late)(lambda: sum_z(2))
    pl.when(late)(lambda: sum_z(3))

    drain()
    slot = z // 2
    act_index = x * 3 + slot
    act_first = (act_index * 32) // 3
    grad_index = jnp.where(slot < 6, (slot - 3) * 4 + x, 12 + (slot - 6) * 3 + x)
    grad_first = (jnp.maximum(grad_index, 0) * 64) // 9
    inverter = (z % 2 == 0) & (y == 0) & ((slot < 6) | late)

    @pl.when(inverter)
    def _():
        wait_bytes(parts, g_recv)
        eye = lax.broadcasted_iota(jnp.int32, (HD, HD), 0) == lax.broadcasted_iota(
            jnp.int32, (HD, HD), 1
        )
        total = parts[0] + parts[1]
        outside, middle = unfold(total[:HALF], total[HALF : HALF + 1])
        trace = jnp.sum(middle, axis=(0, 1), keepdims=True)
        block[...] = (outside + middle) / (trace / HD + 1e-06) + jnp.where(eye, DAMPING, 0.0)
        invert_in_place(block)


    def hand_out(block_index, first_to, count, pieces, window, recv, start):
        def one(i, carry):
            to = first_to + i
            for p in range(pieces):
                if pieces == 2:
                    piece = (3 * to) // 2 + p - 16 * block_index
                else:
                    piece = (9 * to) // 4 + p - 16 * block_index
                use = (piece >= 0) & (piece < 16)
                src = block.at[pl.ds(pl.multiple_of(piece * 8, 8), 8), :]
                dst = window.at[pl.ds(8 * p, 8), :]

                @pl.when(use & (to != dp))
                def _():
                    c = copy(src, dst, w_send.at[p, i], recv.at[p], (to, head))
                    c.start() if start else c.wait_send()

                if start:
                    @pl.when(use & (to == dp))
                    def _():
                        pltpu.make_async_copy(src, dst, recv.at[p]).start()

            return carry

        lax.fori_loop(0, count, one, 0)

    def each_piece(start):
        @pl.when(inverter & (slot < 3))
        def _():
            hand_out(act_index, act_first, 12, 2, act_win, act_recv, start)

        @pl.when(inverter & (slot >= 3))
        def _():
            hand_out(grad_index, grad_first, 9, 3, grad_win, grad_recv, start)

    each_piece(True)
    for s in range(2):
        wait_bytes(act_win.at[pl.ds(8 * s, 8), :], act_recv.at[s])
    for s in range(3):
        wait_bytes(grad_win.at[pl.ds(8 * s, 8), :], grad_recv.at[s])
    rows = act_win[...]
    act_out[...] = jnp.where(dp % 2 == 0, rows[0:12], rows[4:16]).astype(BF16)
    rows = grad_win[...]
    odd = dp % 4
    grad_out[...] = jnp.where(
        odd < 2,
        jnp.where(odd == 0, rows[0:18], rows[2:20]),
        jnp.where(odd == 2, rows[4:22], rows[6:24]),
    ).astype(BF16)

    each_piece(False)


def per_device(queries, key_rows, value_rows, upstream, activations):
    vmem = pl.BlockSpec(memory_space=pltpu.VMEM)
    hbm = pl.BlockSpec(memory_space=pltpu.HBM)
    dma = pltpu.SemaphoreType.DMA
    return pl.pallas_call(
        whole_kernel,
        out_shape=(
            jax.ShapeDtypeStruct((12, HD), BF16),
            jax.ShapeDtypeStruct((18, HD), BF16),
        ),
        in_specs=[hbm] * 5,
        out_specs=(vmem, vmem),
        scratch_shapes=[
            pltpu.VMEM((LEN, 12 * HD), BF16),
            pltpu.VMEM((OWN, 4, LEN, HD), BF16),
            pltpu.VMEM((XN, SLOTS, FOLDED, HD), F32),
            pltpu.VMEM((XN - 1, SLOTS, FOLDED, HD), F32),
            pltpu.VMEM((SLOTS, FOLDED, HD), F32),
            pltpu.VMEM((ZN, SLOTS, 8, HD), F32),
            pltpu.VMEM((SLOTS, 8, HD), F32),
            pltpu.VMEM((YN, FOLDED, HD), F32),
            pltpu.VMEM((HD, HD), F32),
            pltpu.VMEM((16, HD), F32),
            pltpu.VMEM((24, HD), F32),
            dma, dma((OWN,)), dma((OWN,)), dma((OWN,)),
            dma((3,)), dma((18,)), dma((4,)), dma((4,)), dma((4,)), dma((SLOTS,)), dma,
            dma((3, 12)), dma((2,)), dma((3,)),
        ],
        compiler_params=pltpu.CompilerParams(
            collective_id=0, has_side_effects=True, vmem_limit_bytes=54784 * 1024
        ),
        cost_estimate=pl.CostEstimate(
            flops=4_000_000_000, bytes_accessed=5_000_000, transcendentals=1_600_000
        ),
    )(queries, key_rows, value_rows, upstream, activations)


def solution(mesh):
    in_specs = (
        P("dp", None, "head", None),
        P("dp", None, "head", None),
        P("dp", None, "head", None),
        P("dp", None, "head", None),
        P("dp", None, "head"),
    )
    out_specs = (P(("head", "dp"), None), P(("head", "dp"), None))
    return jax.shard_map(
        per_device, mesh=mesh, in_specs=in_specs, out_specs=out_specs, check_vma=False
    )
```

```python
import math

import jax
import jax.numpy as jnp
from jax import lax
from jax.experimental import pallas as pl
from jax.experimental.pallas import tpu as pltpu
from jax.sharding import PartitionSpec as P

DAMPING = 0.1
XN, YN, ZN = 4, 2, 16
GROUP = XN * YN * ZN
HD = 128
LEN = 512
HALF = HD // 2
FOLDED = HALF + 8
PIECES = FOLDED // 8
OWN = 6
QUERIES = 256
PANEL = 64
SLOTS = 8
SCALE = 1.0 / math.sqrt(HD)
LOG2E = 1.4426950408889634
MESH = pl.DeviceIdType.MESH
F32 = jnp.float32
BF16 = jnp.bfloat16


def dot(a, b, a_dim, b_dim):
    return lax.dot_general(a, b, (((a_dim,), (b_dim,)), ((), ())), preferred_element_type=F32)


def head_grams(first_rows, last_rows):
    q, k = first_rows()
    blocks = range(0, LEN, QUERIES)
    probs, probs_half = [], []
    for i in blocks:
        scores = dot(k, q[i : i + QUERIES], 1, 1)
        top = jnp.max(scores, axis=0, keepdims=True)
        weights = jnp.exp2((scores - top) * (SCALE * LOG2E))
        probs.append(weights * (1.0 / jnp.sum(weights, axis=0, keepdims=True)))
        probs_half.append(probs[-1].astype(BF16))
    v, u = last_rows()
    probs_grad = [dot(v, u[i : i + QUERIES], 1, 1) for i in blocks]
    score_grad = []
    for full, half, grad in zip(probs, probs_half, probs_grad):
        row_delta = jnp.sum(half.astype(F32) * grad, axis=0, keepdims=True)
        score_grad.append((full * (grad - row_delta)).astype(BF16))
    value_grad = sum(dot(p, u[i : i + QUERIES], 1, 0) for p, i in zip(probs_half, blocks))
    value_grad = value_grad.astype(BF16)
    yield 2, dot(value_grad, value_grad, 0, 0)
    key_grad = sum(dot(g, q[i : i + QUERIES], 1, 0) for g, i in zip(score_grad, blocks))
    key_grad = (key_grad * SCALE).astype(BF16)
    yield 1, dot(key_grad, key_grad, 0, 0)
    query_grad = [(dot(k, g, 0, 0) * SCALE).astype(BF16) for g in score_grad]
    yield 0, sum(dot(g, g, 1, 1) for g in query_grad)


def fold(block):
    row = lax.broadcasted_iota(jnp.int32, (HALF, HD), 0)
    lane = lax.broadcasted_iota(jnp.int32, (HALF, HD), 1)
    top, bottom = block[:HALF], pltpu.roll(block[HALF:], HALF, 1)
    mixed = jnp.where((lane < HALF) & (lane <= row), bottom, top)
    diagonal = jnp.sum(jnp.where(lane == row, top, 0.0), axis=0, keepdims=True)
    return mixed, jnp.broadcast_to(diagonal, (8, HD))


def unfold(mixed, diagonal):
    row = lax.broadcasted_iota(jnp.int32, (HALF, HD), 0)
    lane = lax.broadcasted_iota(jnp.int32, (HALF, HD), 1)
    turned = pltpu.roll(mixed, HALF, 1)
    upper = jnp.concatenate(
        [
            jnp.where((lane < HALF) & (lane <= row), 0.0, mixed),
            jnp.where((lane >= HALF) & (lane - HALF < row), turned, 0.0),
        ],
        0,
    )
    middle = jnp.concatenate(
        [
            jnp.where(lane == row, diagonal, 0.0),
            jnp.where(lane - HALF == row, turned, 0.0),
        ],
        0,
    )
    return upper + upper.T, middle


def invert_in_place(a_ref):
    lane = lax.broadcasted_iota(jnp.int32, (8, HD), 1)
    row = lax.broadcasted_iota(jnp.int32, (PANEL, HD), 0).reshape(PANEL // 8, 8, HD)
    done = lax.broadcasted_iota(jnp.int32, (HD, HD), 1) < PANEL

    def panel_step(panel, carry):
        rows = pl.ds(pl.multiple_of(panel * PANEL, PANEL), PANEL)
        full = a_ref[...]
        pivots = a_ref[rows, :].reshape(PANEL // 8, 8, HD)
        for s in range(0, PANEL, 2):
            g, r = s // 8, s % 8
            first, second = lane == s, lane == s + 1
            both = first | second

            def spread(i, j):
                return jnp.broadcast_to(
                    pivots[g, r + i : r + i + 1, s + j : s + j + 1], (8, HD)
                )

            a, b, d = spread(0, 0), spread(0, 1), spread(1, 1)
            inv = 1.0 / (a * d - b * b)
            row_a = jnp.broadcast_to(pivots[g, r : r + 1, :], (8, HD))
            row_b = jnp.broadcast_to(pivots[g, r + 1 : r + 2, :], (8, HD))
            row_a = jnp.where(first, 1.0, jnp.where(second, 0.0, row_a))
            row_b = jnp.where(first, 0.0, jnp.where(second, 1.0, row_b))
            new_a = (d * row_a - b * row_b) * inv
            new_b = (a * row_b - b * row_a) * inv
            others = (
                jnp.where(both[None], 0.0, pivots)
                - pivots[:, :, s : s + 1] * new_a[None]
                - pivots[:, :, s + 1 : s + 2] * new_b[None]
            )
            pivots = jnp.where(
                row == s, new_a[None], jnp.where(row == s + 1, new_b[None], others)
            )
        pivots = pivots.reshape(PANEL, HD)
        a_ref[...] = jnp.where(done, 0.0, full) - lax.dot_general(
            full[:, :PANEL], pivots, (((1,), (0,)), ((), ())),
            precision=lax.Precision.HIGHEST, preferred_element_type=F32,
        )
        a_ref[rows, :] = pivots
        a_ref[...] = pltpu.roll(a_ref[...], HD - PANEL, 1)
        return carry

    lax.fori_loop(0, HD // PANEL, panel_step, 0)


def whole_kernel(
    q_hbm, k_hbm, v_hbm, u_hbm, acts_hbm, act_out, grad_out,
    acts, buf, gram, x_in, x_sum, z_in, z_sum, parts, block, act_win, grad_win,
    acts_sem, buf_recv, far_send,
    xa_send, xg_send, x_recv, z_send, z_recv, g_send, g_recv, w_send, act_recv, grad_recv,
):
    tensors = (q_hbm, k_hbm, v_hbm, u_hbm)
    dp = lax.axis_index("dp")
    head = lax.axis_index("head")
    x = dp % XN
    y = (dp // XN) % YN
    z = dp // (XN * YN)
    core = head % 2
    half = head // 2

    def place(z_, y_, x_, head_):
        return (z_ * (XN * YN) + y_ * XN + x_, head_)

    def copy(src, dst, send, recv, device):
        return pltpu.make_async_remote_copy(
            src_ref=src, dst_ref=dst, send_sem=send, recv_sem=recv,
            device_id=device, device_id_type=MESH,
        )

    def wait_bytes(ref, sem):
        pltpu.make_async_copy(ref, ref, sem).wait()

    def rows_of(source):
        return pl.ds(pl.multiple_of(source * HD, HD), HD)

    def start_head(t):
        other = half * 2 + 1 - core
        for i in range(4):
            for to in ((1 - half) * 2, (1 - half) * 2 + 1, other):
                copy(
                    tensors[i].at[0, to * OWN + t], buf.at[t, i, rows_of(head), :],
                    far_send.at[t], buf_recv.at[t, i // 2], place(z, y, x, to),
                ).start()
            pltpu.make_async_copy(
                tensors[i].at[0, head * OWN + t], buf.at[t, i, rows_of(head), :],
                buf_recv.at[t, i // 2],
            ).start()

    stage_slots = ((0, 3), (3, 3), (6, 1), (7, 1))

    def store_gram(owner, slot, value):
        mixed, diagonal = fold(value)
        gram[owner, slot, pl.ds(0, HALF)] = mixed
        gram[owner, slot, pl.ds(HALF, 8)] = diagonal

    def act_copy(r):
        to = (x + r) % XN
        return copy(
            gram.at[to, pl.ds(0, 3)], x_in.at[3 - r, pl.ds(0, 3)],
            xa_send.at[r - 1], x_recv.at[0], place(z, y, to, head),
        )

    def grad_place(t, p):
        n = 3 * t + p
        early = t < 4
        owner = jnp.where(early, n % XN, p)
        slot = jnp.where(early, 3 + n // XN, t + 2)
        stage = jnp.where(early, 1, t - 2)
        return n, owner, slot, stage

    def grad_copy(t, p):
        n, owner, slot, stage = grad_place(t, p)
        r = (x - owner + XN) % XN
        return owner, copy(
            gram.at[owner, slot], x_in.at[jnp.maximum(r - 1, 0), slot],
            xg_send.at[n], x_recv.at[stage], place(z, y, owner, head),
        )

    def compute_head(t):
        def rows(pair):
            wait_bytes(buf.at[t, pl.ds(2 * pair, 2)], buf_recv.at[t, pair])
            return buf[t, 2 * pair], buf[t, 2 * pair + 1]

        for p, block_gram in head_grams(lambda: rows(0), lambda: rows(1)):
            unused, owner, slot, unused = grad_place(t, p)
            store_gram(owner, slot, block_gram)
            owner, send = grad_copy(t, p)
            pl.when(owner != x)(send.start)

    def piece_owner(j):
        return (ZN * j) // PIECES

    my_piece = (PIECES * z + PIECES - 1) // ZN
    holder = piece_owner(my_piece) == z

    def sum_x(stage):
        first, count = stage_slots[stage]
        slots = pl.ds(first, count)
        wait_bytes(x_in.at[:, slots], x_recv.at[stage])
        for s in range(first, first + count):
            x_sum[s] = (gram[x, s] + x_in[0, s]) + (x_in[1, s] + x_in[2, s])
        for j in range(PIECES):
            to = piece_owner(j)
            src, dst = x_sum.at[slots, pl.ds(8 * j, 8), :], z_in.at[z, slots]

            @pl.when(z != to)
            def _():
                copy(
                    src, dst, z_send.at[stage], z_recv.at[stage], place(to, y, x, head)
                ).start()

            @pl.when(z == to)
            def _():
                pltpu.make_async_copy(src, dst, z_recv.at[stage]).start()

    def sum_z(stage):
        first, count = stage_slots[stage]

        @pl.when(holder)
        def _():
            wait_bytes(z_in.at[:, pl.ds(first, count)], z_recv.at[stage])
            for s in range(first, first + count):
                z_sum[s] = jnp.sum(z_in[:, s], axis=0)
                dst = parts.at[y, pl.ds(pl.multiple_of(my_piece * 8, 8), 8), :]
                mine = (z == 2 * s) & (y == 0)

                @pl.when(jnp.logical_not(mine))
                def _():
                    copy(
                        z_sum.at[s], dst, g_send.at[s], g_recv, place(2 * s, 0, x, head)
                    ).start()

                @pl.when(mine)
                def _():
                    pltpu.make_async_copy(z_sum.at[s], dst, g_recv).start()

    late = x < 3

    def drain():
        def sent(t, carry):
            wait_bytes(buf.at[t, :, pl.ds(0, 3 * HD), :], far_send.at[t])
            for p in range(3):
                owner, send = grad_copy(t, p)
                pl.when(owner != x)(send.wait_send)
            return carry

        lax.fori_loop(0, OWN, sent, 0)
        for r in (1, 3, 2):
            act_copy(r).wait_send()
        for stage, (first, count) in enumerate(stage_slots):
            def drain_stage():
                @pl.when(holder)
                def _():
                    wait_bytes(
                        z_in.at[pl.ds(0, PIECES - 1), pl.ds(first, count)], z_send.at[stage]
                    )
                    for s in range(first, first + count):
                        @pl.when(jnp.logical_not((z == 2 * s) & (y == 0)))
                        def _():
                            wait_bytes(z_sum.at[s], g_send.at[s])

                @pl.when(jnp.logical_not(holder))
                def _():
                    wait_bytes(z_in.at[pl.ds(0, PIECES), pl.ds(first, count)], z_send.at[stage])

            drain_stage() if stage < 2 else pl.when(late)(drain_stage)

    load = pltpu.make_async_copy(acts_hbm.at[0], acts, acts_sem)
    load.start()

    barrier = pltpu.get_barrier_semaphore()
    for r in range(1, 4):
        pl.semaphore_signal(
            barrier, inc=1, device_id=(dp, (head + r) % 4), device_id_type=MESH
        )

    def greet(r, carry):
        pl.semaphore_signal(
            barrier, inc=1, device_id=((dp + r) % GROUP, head), device_id_type=MESH
        )
        return carry

    lax.fori_loop(1, GROUP, greet, 0)
    pl.semaphore_wait(barrier, GROUP - 1 + 3)
    for t in range(3):
        start_head(t)
    load.wait()

    def act_gram(b, carry):
        item = acts[:, pl.ds(pl.multiple_of(b * HD, HD), HD)]
        store_gram(b // 3, b % 3, dot(item, item, 0, 0))
        return carry

    lax.fori_loop(0, 12, act_gram, 0)
    for r in (2, 1, 3):
        act_copy(r).start()

    def step(t, carry):
        @pl.when(t + 2 < OWN)
        def _():
            start_head(t + 2)

        @pl.when(t == 3)
        def _():
            sum_x(0)

        @pl.when(t == 5)
        def _():
            sum_z(0)

        compute_head(t - 1)

        @pl.when(t == 5)
        def _():
            sum_x(1)

        return carry

    lax.fori_loop(1, OWN + 1, step, 0)
    pl.when(late)(lambda: sum_x(2))
    sum_z(1)
    pl.when(late)(lambda: sum_x(3))
    pl.when(late)(lambda: sum_z(2))
    pl.when(late)(lambda: sum_z(3))

    drain()
    slot = z // 2
    act_index = x * 3 + slot
    act_first = (act_index * 32) // 3
    grad_index = jnp.where(slot < 6, (slot - 3) * 4 + x, 12 + (slot - 6) * 3 + x)
    grad_first = (jnp.maximum(grad_index, 0) * 64) // 9
    inverter = (z % 2 == 0) & (y == 0) & ((slot < 6) | late)

    @pl.when(inverter)
    def _():
        wait_bytes(parts, g_recv)
        eye = lax.broadcasted_iota(jnp.int32, (HD, HD), 0) == lax.broadcasted_iota(
            jnp.int32, (HD, HD), 1
        )
        total = parts[0] + parts[1]
        outside, middle = unfold(total[:HALF], total[HALF : HALF + 1])
        trace = jnp.sum(middle, axis=(0, 1), keepdims=True)
        block[...] = (outside + middle) / (trace / HD + 1e-06) + jnp.where(eye, DAMPING, 0.0)
        invert_in_place(block)


    def hand_out(block_index, first_to, count, pieces, window, recv, start):
        def one(i, carry):
            to = first_to + i
            for p in range(pieces):
                if pieces == 2:
                    piece = (3 * to) // 2 + p - 16 * block_index
                else:
                    piece = (9 * to) // 4 + p - 16 * block_index
                use = (piece >= 0) & (piece < 16)
                src = block.at[pl.ds(pl.multiple_of(piece * 8, 8), 8), :]
                dst = window.at[pl.ds(8 * p, 8), :]

                @pl.when(use & (to != dp))
                def _():
                    c = copy(src, dst, w_send.at[p, i], recv.at[p], (to, head))
                    c.start() if start else c.wait_send()

                if start:
                    @pl.when(use & (to == dp))
                    def _():
                        pltpu.make_async_copy(src, dst, recv.at[p]).start()

            return carry

        lax.fori_loop(0, count, one, 0)

    def each_piece(start):
        @pl.when(inverter & (slot < 3))
        def _():
            hand_out(act_index, act_first, 12, 2, act_win, act_recv, start)

        @pl.when(inverter & (slot >= 3))
        def _():
            hand_out(grad_index, grad_first, 9, 3, grad_win, grad_recv, start)

    each_piece(True)
    for s in range(2):
        wait_bytes(act_win.at[pl.ds(8 * s, 8), :], act_recv.at[s])
    for s in range(3):
        wait_bytes(grad_win.at[pl.ds(8 * s, 8), :], grad_recv.at[s])
    rows = act_win[...]
    act_out[...] = jnp.where(dp % 2 == 0, rows[0:12], rows[4:16]).astype(BF16)
    rows = grad_win[...]
    odd = dp % 4
    grad_out[...] = jnp.where(
        odd < 2,
        jnp.where(odd == 0, rows[0:18], rows[2:20]),
        jnp.where(odd == 2, rows[4:22], rows[6:24]),
    ).astype(BF16)

    each_piece(False)


def per_device(queries, key_rows, value_rows, upstream, activations):
    vmem = pl.BlockSpec(memory_space=pltpu.VMEM)
    hbm = pl.BlockSpec(memory_space=pltpu.HBM)
    dma = pltpu.SemaphoreType.DMA
    return pl.pallas_call(
        whole_kernel,
        out_shape=(
            jax.ShapeDtypeStruct((12, HD), BF16),
            jax.ShapeDtypeStruct((18, HD), BF16),
        ),
        in_specs=[hbm] * 5,
        out_specs=(vmem, vmem),
        scratch_shapes=[
            pltpu.VMEM((LEN, 12 * HD), BF16),
            pltpu.VMEM((OWN, 4, LEN, HD), BF16),
            pltpu.VMEM((XN, SLOTS, FOLDED, HD), F32),
            pltpu.VMEM((XN - 1, SLOTS, FOLDED, HD), F32),
            pltpu.VMEM((SLOTS, FOLDED, HD), F32),
            pltpu.VMEM((ZN, SLOTS, 8, HD), F32),
            pltpu.VMEM((SLOTS, 8, HD), F32),
            pltpu.VMEM((YN, FOLDED, HD), F32),
            pltpu.VMEM((HD, HD), F32),
            pltpu.VMEM((16, HD), F32),
            pltpu.VMEM((24, HD), F32),
            dma, dma((OWN, 2)), dma((OWN,)),
            dma((3,)), dma((18,)), dma((4,)), dma((4,)), dma((4,)), dma((SLOTS,)), dma,
            dma((3, 12)), dma((2,)), dma((3,)),
        ],
        compiler_params=pltpu.CompilerParams(
            collective_id=0, has_side_effects=True, vmem_limit_bytes=54784 * 1024
        ),
        cost_estimate=pl.CostEstimate(
            flops=4_000_000_000, bytes_accessed=5_000_000, transcendentals=1_600_000
        ),
    )(queries, key_rows, value_rows, upstream, activations)


def solution(mesh):
    in_specs = (
        P("dp", None, "head", None),
        P("dp", None, "head", None),
        P("dp", None, "head", None),
        P("dp", None, "head", None),
        P("dp", None, "head"),
    )
    out_specs = (P(("head", "dp"), None), P(("head", "dp"), None))
    return jax.shard_map(
        per_device, mesh=mesh, in_specs=in_specs, out_specs=out_specs, check_vma=False
    )
```

```python
import math

import jax
import jax.numpy as jnp
from jax import lax
from jax.experimental import pallas as pl
from jax.experimental.pallas import tpu as pltpu
from jax.sharding import PartitionSpec as P

DAMPING = 0.1
XN, YN, ZN = 4, 2, 16
GROUP = XN * YN * ZN
HD = 128
LEN = 512
HALF = HD // 2
FOLDED = HALF + 8
PIECES = FOLDED // 8
OWN = 6
QUERIES = 256
PANEL = 64
SLOTS = 8
SCALE = 1.0 / math.sqrt(HD)
LOG2E = 1.4426950408889634
MESH = pl.DeviceIdType.MESH
F32 = jnp.float32
BF16 = jnp.bfloat16


def dot(a, b, a_dim, b_dim):
    return lax.dot_general(a, b, (((a_dim,), (b_dim,)), ((), ())), preferred_element_type=F32)


def head_grams(first_rows, last_rows):
    q, k = first_rows()
    blocks = range(0, LEN, QUERIES)
    probs, probs_half = [], []
    for i in blocks:
        scores = dot(k, q[i : i + QUERIES], 1, 1)
        top = jnp.max(scores, axis=0, keepdims=True)
        weights = jnp.exp2((scores - top) * (SCALE * LOG2E))
        probs.append(weights * (1.0 / jnp.sum(weights, axis=0, keepdims=True)))
        probs_half.append(probs[-1].astype(BF16))
    v, u = last_rows()
    probs_grad = [dot(v, u[i : i + QUERIES], 1, 1) for i in blocks]
    score_grad = []
    for full, half, grad in zip(probs, probs_half, probs_grad):
        row_delta = jnp.sum(half.astype(F32) * grad, axis=0, keepdims=True)
        score_grad.append((full * (grad - row_delta)).astype(BF16))
    value_grad = sum(dot(p, u[i : i + QUERIES], 1, 0) for p, i in zip(probs_half, blocks))
    value_grad = value_grad.astype(BF16)
    yield 2, dot(value_grad, value_grad, 0, 0)
    key_grad = sum(dot(g, q[i : i + QUERIES], 1, 0) for g, i in zip(score_grad, blocks))
    key_grad = (key_grad * SCALE).astype(BF16)
    yield 1, dot(key_grad, key_grad, 0, 0)
    query_grad = [(dot(k, g, 0, 0) * SCALE).astype(BF16) for g in score_grad]
    yield 0, sum(dot(g, g, 1, 1) for g in query_grad)


def fold(block):
    row = lax.broadcasted_iota(jnp.int32, (HALF, HD), 0)
    lane = lax.broadcasted_iota(jnp.int32, (HALF, HD), 1)
    top, bottom = block[:HALF], pltpu.roll(block[HALF:], HALF, 1)
    mixed = jnp.where((lane < HALF) & (lane <= row), bottom, top)
    diagonal = jnp.sum(jnp.where(lane == row, top, 0.0), axis=0, keepdims=True)
    return mixed, jnp.broadcast_to(diagonal, (8, HD))


def unfold(mixed, diagonal):
    row = lax.broadcasted_iota(jnp.int32, (HALF, HD), 0)
    lane = lax.broadcasted_iota(jnp.int32, (HALF, HD), 1)
    turned = pltpu.roll(mixed, HALF, 1)
    upper = jnp.concatenate(
        [
            jnp.where((lane < HALF) & (lane <= row), 0.0, mixed),
            jnp.where((lane >= HALF) & (lane - HALF < row), turned, 0.0),
        ],
        0,
    )
    middle = jnp.concatenate(
        [
            jnp.where(lane == row, diagonal, 0.0),
            jnp.where(lane - HALF == row, turned, 0.0),
        ],
        0,
    )
    return upper + upper.T, middle


def invert_in_place(a_ref):
    lane = lax.broadcasted_iota(jnp.int32, (8, HD), 1)
    row = lax.broadcasted_iota(jnp.int32, (PANEL, HD), 0).reshape(PANEL // 8, 8, HD)
    done = lax.broadcasted_iota(jnp.int32, (HD, HD), 1) < PANEL

    def panel_step(panel, carry):
        rows = pl.ds(pl.multiple_of(panel * PANEL, PANEL), PANEL)
        full = a_ref[...]
        pivots = a_ref[rows, :].reshape(PANEL // 8, 8, HD)
        for s in range(0, PANEL, 2):
            g, r = s // 8, s % 8
            first, second = lane == s, lane == s + 1
            both = first | second

            def spread(i, j):
                return jnp.broadcast_to(
                    pivots[g, r + i : r + i + 1, s + j : s + j + 1], (8, HD)
                )

            a, b, d = spread(0, 0), spread(0, 1), spread(1, 1)
            inv = 1.0 / (a * d - b * b)
            row_a = jnp.broadcast_to(pivots[g, r : r + 1, :], (8, HD))
            row_b = jnp.broadcast_to(pivots[g, r + 1 : r + 2, :], (8, HD))
            row_a = jnp.where(first, 1.0, jnp.where(second, 0.0, row_a))
            row_b = jnp.where(first, 0.0, jnp.where(second, 1.0, row_b))
            new_a = (d * row_a - b * row_b) * inv
            new_b = (a * row_b - b * row_a) * inv
            others = (
                jnp.where(both[None], 0.0, pivots)
                - pivots[:, :, s : s + 1] * new_a[None]
                - pivots[:, :, s + 1 : s + 2] * new_b[None]
            )
            pivots = jnp.where(
                row == s, new_a[None], jnp.where(row == s + 1, new_b[None], others)
            )
        pivots = pivots.reshape(PANEL, HD)
        a_ref[...] = jnp.where(done, 0.0, full) - lax.dot_general(
            full[:, :PANEL], pivots, (((1,), (0,)), ((), ())),
            precision=lax.Precision.HIGHEST, preferred_element_type=F32,
        )
        a_ref[rows, :] = pivots
        a_ref[...] = pltpu.roll(a_ref[...], HD - PANEL, 1)
        return carry

    lax.fori_loop(0, HD // PANEL, panel_step, 0)


def whole_kernel(
    q_hbm, k_hbm, v_hbm, u_hbm, acts_hbm, act_out, grad_out,
    acts, buf, gram, x_in, x_sum, z_in, z_sum, parts, block, act_win, grad_win,
    acts_sem, buf_recv, far_send,
    xa_send, xg_send, x_recv, z_send, z_recv, g_send, g_recv, w_send, act_recv, grad_recv,
    staged, staged_sem,
):
    dp = lax.axis_index("dp")
    head = lax.axis_index("head")
    x = dp % XN
    y = (dp // XN) % YN
    z = dp // (XN * YN)
    core = head % 2
    half = head // 2

    def place(z_, y_, x_, head_):
        return (z_ * (XN * YN) + y_ * XN + x_, head_)

    def copy(src, dst, send, recv, device):
        return pltpu.make_async_remote_copy(
            src_ref=src, dst_ref=dst, send_sem=send, recv_sem=recv,
            device_id=device, device_id_type=MESH,
        )

    def wait_bytes(ref, sem):
        pltpu.make_async_copy(ref, ref, sem).wait()

    def rows_of(source):
        return pl.ds(pl.multiple_of(source * HD, HD), HD)

    def start_head(t):
        other = half * 2 + 1 - core
        for i in range(4):
            for to in ((1 - half) * 2, (1 - half) * 2 + 1, other):
                copy(
                    staged.at[i, to * OWN + t], buf.at[t, i, rows_of(head), :],
                    far_send.at[t], buf_recv.at[t, i // 2], place(z, y, x, to),
                ).start()
            pltpu.make_async_copy(
                staged.at[i, head * OWN + t], buf.at[t, i, rows_of(head), :],
                buf_recv.at[t, i // 2],
            ).start()

    stage_slots = ((0, 3), (3, 3), (6, 1), (7, 1))

    def store_gram(owner, slot, value):
        mixed, diagonal = fold(value)
        gram[owner, slot, pl.ds(0, HALF)] = mixed
        gram[owner, slot, pl.ds(HALF, 8)] = diagonal

    def act_copy(r):
        to = (x + r) % XN
        return copy(
            gram.at[to, pl.ds(0, 3)], x_in.at[3 - r, pl.ds(0, 3)],
            xa_send.at[r - 1], x_recv.at[0], place(z, y, to, head),
        )

    def grad_place(t, p):
        n = 3 * t + p
        early = t < 4
        owner = jnp.where(early, n % XN, p)
        slot = jnp.where(early, 3 + n // XN, t + 2)
        stage = jnp.where(early, 1, t - 2)
        return n, owner, slot, stage

    def grad_copy(t, p):
        n, owner, slot, stage = grad_place(t, p)
        r = (x - owner + XN) % XN
        return owner, copy(
            gram.at[owner, slot], x_in.at[jnp.maximum(r - 1, 0), slot],
            xg_send.at[n], x_recv.at[stage], place(z, y, owner, head),
        )

    def compute_head(t):
        def rows(pair):
            wait_bytes(buf.at[t, pl.ds(2 * pair, 2)], buf_recv.at[t, pair])
            return buf[t, 2 * pair], buf[t, 2 * pair + 1]

        for p, block_gram in head_grams(lambda: rows(0), lambda: rows(1)):
            unused, owner, slot, unused = grad_place(t, p)
            store_gram(owner, slot, block_gram)
            owner, send = grad_copy(t, p)
            pl.when(owner != x)(send.start)

    def piece_owner(j):
        return (ZN * j) // PIECES

    my_piece = (PIECES * z + PIECES - 1) // ZN
    holder = piece_owner(my_piece) == z

    def sum_x(stage):
        first, count = stage_slots[stage]
        slots = pl.ds(first, count)
        wait_bytes(x_in.at[:, slots], x_recv.at[stage])
        for s in range(first, first + count):
            x_sum[s] = (gram[x, s] + x_in[0, s]) + (x_in[1, s] + x_in[2, s])
        for j in range(PIECES):
            to = piece_owner(j)
            src, dst = x_sum.at[slots, pl.ds(8 * j, 8), :], z_in.at[z, slots]

            @pl.when(z != to)
            def _():
                copy(
                    src, dst, z_send.at[stage], z_recv.at[stage], place(to, y, x, head)
                ).start()

            @pl.when(z == to)
            def _():
                pltpu.make_async_copy(src, dst, z_recv.at[stage]).start()

    def sum_z(stage):
        first, count = stage_slots[stage]

        @pl.when(holder)
        def _():
            wait_bytes(z_in.at[:, pl.ds(first, count)], z_recv.at[stage])
            for s in range(first, first + count):
                z_sum[s] = jnp.sum(z_in[:, s], axis=0)
                dst = parts.at[y, pl.ds(pl.multiple_of(my_piece * 8, 8), 8), :]
                mine = (z == 2 * s) & (y == 0)

                @pl.when(jnp.logical_not(mine))
                def _():
                    copy(
                        z_sum.at[s], dst, g_send.at[s], g_recv, place(2 * s, 0, x, head)
                    ).start()

                @pl.when(mine)
                def _():
                    pltpu.make_async_copy(z_sum.at[s], dst, g_recv).start()

    late = x < 3

    def drain():
        def sent(t, carry):
            wait_bytes(buf.at[t, :, pl.ds(0, 3 * HD), :], far_send.at[t])
            for p in range(3):
                owner, send = grad_copy(t, p)
                pl.when(owner != x)(send.wait_send)
            return carry

        lax.fori_loop(0, OWN, sent, 0)
        for r in (1, 3, 2):
            act_copy(r).wait_send()
        for stage, (first, count) in enumerate(stage_slots):
            def drain_stage():
                @pl.when(holder)
                def _():
                    wait_bytes(
                        z_in.at[pl.ds(0, PIECES - 1), pl.ds(first, count)], z_send.at[stage]
                    )
                    for s in range(first, first + count):
                        @pl.when(jnp.logical_not((z == 2 * s) & (y == 0)))
                        def _():
                            wait_bytes(z_sum.at[s], g_send.at[s])

                @pl.when(jnp.logical_not(holder))
                def _():
                    wait_bytes(z_in.at[pl.ds(0, PIECES), pl.ds(first, count)], z_send.at[stage])

            drain_stage() if stage < 2 else pl.when(late)(drain_stage)

    load = pltpu.make_async_copy(acts_hbm.at[0], acts, acts_sem)
    stage = [
        pltpu.make_async_copy(ref.at[0], staged.at[i], staged_sem.at[i])
        for i, ref in enumerate((q_hbm, k_hbm, v_hbm, u_hbm))
    ]
    for item in stage:
        item.start()
    load.start()

    barrier = pltpu.get_barrier_semaphore()
    for r in range(1, 4):
        pl.semaphore_signal(
            barrier, inc=1, device_id=(dp, (head + r) % 4), device_id_type=MESH
        )

    def greet(r, carry):
        pl.semaphore_signal(
            barrier, inc=1, device_id=((dp + r) % GROUP, head), device_id_type=MESH
        )
        return carry

    lax.fori_loop(1, GROUP, greet, 0)
    for item in stage:
        item.wait()
    pl.semaphore_wait(barrier, GROUP - 1 + 3)
    for t in range(3):
        start_head(t)
    load.wait()

    def act_gram(b, carry):
        item = acts[:, pl.ds(pl.multiple_of(b * HD, HD), HD)]
        store_gram(b // 3, b % 3, dot(item, item, 0, 0))
        return carry

    lax.fori_loop(0, 12, act_gram, 0)
    for r in (2, 1, 3):
        act_copy(r).start()

    def step(t, carry):
        @pl.when(t + 2 < OWN)
        def _():
            start_head(t + 2)

        @pl.when(t == 3)
        def _():
            sum_x(0)

        @pl.when(t == 5)
        def _():
            sum_z(0)

        compute_head(t - 1)

        @pl.when(t == 5)
        def _():
            sum_x(1)

        return carry

    lax.fori_loop(1, OWN + 1, step, 0)
    pl.when(late)(lambda: sum_x(2))
    sum_z(1)
    pl.when(late)(lambda: sum_x(3))
    pl.when(late)(lambda: sum_z(2))
    pl.when(late)(lambda: sum_z(3))

    drain()
    slot = z // 2
    act_index = x * 3 + slot
    act_first = (act_index * 32) // 3
    grad_index = jnp.where(slot < 6, (slot - 3) * 4 + x, 12 + (slot - 6) * 3 + x)
    grad_first = (jnp.maximum(grad_index, 0) * 64) // 9
    inverter = (z % 2 == 0) & (y == 0) & ((slot < 6) | late)

    @pl.when(inverter)
    def _():
        wait_bytes(parts, g_recv)
        eye = lax.broadcasted_iota(jnp.int32, (HD, HD), 0) == lax.broadcasted_iota(
            jnp.int32, (HD, HD), 1
        )
        total = parts[0] + parts[1]
        outside, middle = unfold(total[:HALF], total[HALF : HALF + 1])
        trace = jnp.sum(middle, axis=(0, 1), keepdims=True)
        block[...] = (outside + middle) / (trace / HD + 1e-06) + jnp.where(eye, DAMPING, 0.0)
        invert_in_place(block)


    def hand_out(block_index, first_to, count, pieces, window, recv, start):
        def one(i, carry):
            to = first_to + i
            for p in range(pieces):
                if pieces == 2:
                    piece = (3 * to) // 2 + p - 16 * block_index
                else:
                    piece = (9 * to) // 4 + p - 16 * block_index
                use = (piece >= 0) & (piece < 16)
                src = block.at[pl.ds(pl.multiple_of(piece * 8, 8), 8), :]
                dst = window.at[pl.ds(8 * p, 8), :]

                @pl.when(use & (to != dp))
                def _():
                    c = copy(src, dst, w_send.at[p, i], recv.at[p], (to, head))
                    c.start() if start else c.wait_send()

                if start:
                    @pl.when(use & (to == dp))
                    def _():
                        pltpu.make_async_copy(src, dst, recv.at[p]).start()

            return carry

        lax.fori_loop(0, count, one, 0)

    def each_piece(start):
        @pl.when(inverter & (slot < 3))
        def _():
            hand_out(act_index, act_first, 12, 2, act_win, act_recv, start)

        @pl.when(inverter & (slot >= 3))
        def _():
            hand_out(grad_index, grad_first, 9, 3, grad_win, grad_recv, start)

    each_piece(True)
    for s in range(2):
        wait_bytes(act_win.at[pl.ds(8 * s, 8), :], act_recv.at[s])
    for s in range(3):
        wait_bytes(grad_win.at[pl.ds(8 * s, 8), :], grad_recv.at[s])
    rows = act_win[...]
    act_out[...] = jnp.where(dp % 2 == 0, rows[0:12], rows[4:16]).astype(BF16)
    rows = grad_win[...]
    odd = dp % 4
    grad_out[...] = jnp.where(
        odd < 2,
        jnp.where(odd == 0, rows[0:18], rows[2:20]),
        jnp.where(odd == 2, rows[4:22], rows[6:24]),
    ).astype(BF16)

    each_piece(False)


def per_device(queries, key_rows, value_rows, upstream, activations):
    vmem = pl.BlockSpec(memory_space=pltpu.VMEM)
    hbm = pl.BlockSpec(memory_space=pltpu.HBM)
    dma = pltpu.SemaphoreType.DMA
    return pl.pallas_call(
        whole_kernel,
        out_shape=(
            jax.ShapeDtypeStruct((12, HD), BF16),
            jax.ShapeDtypeStruct((18, HD), BF16),
        ),
        in_specs=[hbm] * 5,
        out_specs=(vmem, vmem),
        scratch_shapes=[
            pltpu.VMEM((LEN, 12 * HD), BF16),
            pltpu.VMEM((OWN, 4, LEN, HD), BF16),
            pltpu.VMEM((XN, SLOTS, FOLDED, HD), F32),
            pltpu.VMEM((XN - 1, SLOTS, FOLDED, HD), F32),
            pltpu.VMEM((SLOTS, FOLDED, HD), F32),
            pltpu.VMEM((ZN, SLOTS, 8, HD), F32),
            pltpu.VMEM((SLOTS, 8, HD), F32),
            pltpu.VMEM((YN, FOLDED, HD), F32),
            pltpu.VMEM((HD, HD), F32),
            pltpu.VMEM((16, HD), F32),
            pltpu.VMEM((24, HD), F32),
            dma, dma((OWN, 2)), dma((OWN,)),
            dma((3,)), dma((18,)), dma((4,)), dma((4,)), dma((4,)), dma((SLOTS,)), dma,
            dma((3, 12)), dma((2,)), dma((3,)),
            pltpu.VMEM((4, 4 * OWN, HD, HD), BF16), dma((4,)),
        ],
        compiler_params=pltpu.CompilerParams(
            collective_id=0, has_side_effects=True, vmem_limit_bytes=54784 * 1024
        ),
        cost_estimate=pl.CostEstimate(
            flops=4_000_000_000, bytes_accessed=5_000_000, transcendentals=1_600_000
        ),
    )(queries, key_rows, value_rows, upstream, activations)


def solution(mesh):
    in_specs = (
        P("dp", None, "head", None),
        P("dp", None, "head", None),
        P("dp", None, "head", None),
        P("dp", None, "head", None),
        P("dp", None, "head"),
    )
    out_specs = (P(("head", "dp"), None), P(("head", "dp"), None))
    return jax.shard_map(
        per_device, mesh=mesh, in_specs=in_specs, out_specs=out_specs, check_vma=False
    )
```
